32 devices in a mesh: sec: 8 (over z, x), row: 4 (over y, core).
Axes of the slice: x: 2, y: 2, z: 4, core: 2. Of those that a mesh axis runs over, the one named last changes fastest.
Arguments:
- corner_ul: bfloat16 [8, 1024, 1024], P('sec', 'row'), may hold values from -6 to 6
- corner_ur: bfloat16 [8, 1024, 1024], P('sec'), may hold values from -0.1875 to 0.1875
- corner_dl: bfloat16 [8, 1024, 1024], P('sec', 'row'), may hold values from -6 to 6
- corner_dr: bfloat16 [8, 1024, 1024], P('sec'), may hold values from -0.1875 to 0.1875
- left_factor: bfloat16 [8, 1024, 16], P('sec', 'row'), may hold values from -0.1875 to 0.1875
- right_factor: bfloat16 [8, 1024, 16], P('sec', 'row'), may hold values from -0.1875 to 0.1875
- singular: float32 [8, 16], P('sec'), may hold values from 0.25 to 4
- states: int32 [8], P('sec'), may hold values from 8 to 16, as said below
- kept: int32 [8], P('sec'), may hold values from 8 to 16, as said below
- joining_map: int32 [8, 16], P('sec'), may hold values from 0 to 15, each once within a row
Outputs:
- proj_tilde: bfloat16 [8, 1024, 16], P('sec', 'row')
- proj: bfloat16 [8, 1024, 16], P('sec', 'row')
- intersection: float32 [8, 16, 16], P('sec')
The draws below stay inside these ranges and needn't reach their ends.
Inputs may be any that keep to these rules, and one draw needn't show every extreme that they name: `states`: at least half of 16; some sector has all 16. `kept`: at least half of 16; some sector keeps all 16. `joining_map`: each row is a permutation of 0 to 15.
All inputs are finite; a program needn't handle non-finite values.
Results may differ from the reference program's by a relative error of at most 0.0051.
Values may be sent and summed in bfloat16 or wider, within the bound.
No kernel may reach another device: no remote copies, remote signals or barrier semaphores. Data moves between devices by JAX's collectives and lax.ppermute only.
A program may use at most 64 MiB of HBM per device.

```python
import math
import jax
import jax.numpy as jnp
from jax import lax

DD = 64
CHS = 16
KS = 16
DS = 1024
SECTORS = 8


def draw_states(key, part):
    first = jax.random.fold_in(key, 11)
    second = jax.random.fold_in(key, 12)
    values = jax.random.randint(first, (SECTORS,), (CHS + 1) // 2, CHS + 1)
    where_full = jax.random.randint(second, (), 0, SECTORS)
    return values.at[where_full].set(CHS).astype(jnp.int32)


def draw_kept(key, part):
    first = jax.random.fold_in(key, 21)
    second = jax.random.fold_in(key, 22)
    values = jax.random.randint(first, (SECTORS,), (KS + 1) // 2, KS + 1)
    where_full = jax.random.randint(second, (), 0, SECTORS)
    return values.at[where_full].set(KS).astype(jnp.int32)


def block_levels(key, dims, cuts, smallest, high):
    def one(dim, shards_of):
        steps = jax.random.uniform(jax.random.fold_in(jax.random.fold_in(key, 6), dim), (shards_of,), jnp.float32, smallest / len(cuts), high / len(cuts))
        return jnp.repeat(jnp.exp(steps), dims[dim] // shards_of).reshape((-1,) + (1,) * (len(dims) - dim - 1))

    gain = one(*cuts[0])
    for cut in cuts[1:]:
        gain = gain * one(*cut)
    return gain


def gaussian(rng, dims, width, bound, split=(), held_as=jnp.bfloat16):
    factor_of = block_levels(rng, dims, split, -0.22, 0.18) if split else 1.0
    result = jax.random.normal(rng, dims, jnp.float32) * width * factor_of
    return jnp.minimum(jnp.maximum(result, -bound), bound).astype(held_as)


def setup_inputs(seed: int = 0) -> dict:
    splits = jax.random.split(jax.random.key(seed), 11)
    return {
        "corner_ul": gaussian(splits[0], (SECTORS, DS, DS), 1.0, 6.0, ((0, 8), (1, 4))),
        "corner_ur": gaussian(splits[1], (SECTORS, DS, DS), DS ** -0.5, 0.1875, ((0, 8),)),
        "corner_dl": gaussian(splits[2], (SECTORS, DS, DS), 1.0, 6.0, ((0, 8), (1, 4))),
        "corner_dr": gaussian(splits[3], (SECTORS, DS, DS), DS ** -0.5, 0.1875, ((0, 8),)),
        "left_factor": gaussian(splits[4], (SECTORS, DS, KS), DS ** -0.5, 0.1875, ((0, 8), (1, 4))),
        "right_factor": gaussian(splits[5], (SECTORS, DS, KS), DS ** -0.5, 0.1875, ((0, 8), (1, 4))),
        "singular": jnp.clip(jnp.exp(math.log(4.0) - 2.7725887 * jax.random.uniform(splits[6], (SECTORS, KS), jnp.float32) ** block_levels(splits[6], (SECTORS, KS), ((0, 8),), -0.2, 0.2)), 0.25, 4.0),
        "states": draw_states(jax.random.fold_in(splits[10], 71), 0),
        "kept": draw_kept(jax.random.fold_in(splits[10], 71), 0),
        "joining_map": jax.vmap(lambda own: jax.random.permutation(own, CHS))(jax.random.split(splits[9], SECTORS)).reshape((SECTORS, CHS)).astype(jnp.int32),
    }


def regroup(block, order):
    four = block.reshape(DD, CHS, DD, CHS)
    four = jnp.take(four, order, axis=1)
    return jnp.transpose(four, (2, 1, 0, 3)).reshape(DS, DS)

def reference(corner_ul, corner_ur, corner_dl, corner_dr, left_factor, right_factor, singular, states, kept, joining_map):
    live_base = jnp.arange(DS, dtype=jnp.int32) % CHS

    def half(pieces):
        left, right, count = pieces
        live = (live_base < count).astype(jnp.float32)
        full = jnp.dot(left, right, preferred_element_type=jnp.float32)
        return (full * live[:, None] * live[None, :]).astype(jnp.bfloat16)
    upper = lax.map(half, (corner_ul, corner_ur, states))
    lower = lax.map(half, (corner_dl, corner_dr, states))
    sector_ids = jnp.arange(SECTORS, dtype=jnp.int32)

    def project(sector):
        up_src = upper[(sector - 1) % SECTORS]
        low_src = lower[(sector + 1) % SECTORS]
        r_left = regroup(up_src, joining_map[sector])
        r_right = regroup(low_src, joining_map[sector])
        a_half = jnp.dot(r_left.T, left_factor[sector], preferred_element_type=jnp.float32)
        b_half = jnp.dot(r_right.T, right_factor[sector], preferred_element_type=jnp.float32)
        columns = jnp.arange(KS, dtype=jnp.int32)
        weight = jnp.where(columns < kept[sector], 1.0 / jnp.sqrt(singular[sector]), 0.0).astype(jnp.float32)
        scaled_a = a_half * weight[None, :]
        scaled_b = b_half * weight[None, :]
        intersection = jnp.dot(scaled_a.T, scaled_b, precision=lax.Precision.HIGHEST, preferred_element_type=jnp.float32)
        intersection = intersection / jnp.sqrt(jnp.float32(DS))
        return (scaled_a.astype(jnp.bfloat16), scaled_b.astype(jnp.bfloat16), intersection)
    proj_tilde, proj, intersection = lax.map(project, sector_ids)
    return (proj_tilde, proj, intersection)
```

```python
import functools

import jax
import jax.numpy as jnp
from jax import lax
from jax.experimental import pallas as pl
from jax.experimental.pallas import tpu as pltpu
from jax.sharding import PartitionSpec as P

LANES = 128
F32, BF16 = jnp.float32, jnp.bfloat16
VMEM_BYTES = 24 * 1024 * 1024


def iota(shape, dim):
    return lax.broadcasted_iota(jnp.int32, shape, dim)


def is_upper():
    return lax.axis_index("row") % 2 == 1


def order_kernel(map_ref, u_ref, u_got_ref, v_ref, v_got_ref, out_ref):
    states_here = map_ref.shape[1]
    lane = iota((LANES, LANES), 1)
    row = iota((LANES, LANES), 0)
    wanted = jnp.zeros((LANES, LANES), jnp.int32)
    for x in range(states_here):
        wanted = jnp.where(lane % states_here == map_ref[0, x], x, wanted)
    same_bond = row // states_here == lane // states_here
    mover = jnp.where(same_bond & (row % states_here == wanted), 1.0, 0.0).astype(BF16)
    mine = is_upper()
    first = jnp.where(mine, u_got_ref[...], v_ref[...])
    second = jnp.where(mine, u_ref[...], v_got_ref[...])
    both = jnp.concatenate([first, second], axis=1)
    for start in range(0, both.shape[1], LANES):
        moved = jnp.dot(both[:, start : start + LANES], mover, preferred_element_type=F32)
        out_ref[:, start : start + LANES] = moved.astype(BF16)


def half_kernel(states_ref, ul, ul_got, ur, dl, dl_got, dr, out_ref, left, right, sems, *, parts, states_here):
    rows, width = ul.shape
    step = width // parts
    mine = is_upper()

    def copies(first, second, matrix):
        todo = [
            pltpu.make_async_copy(first, left.at[pl.ds(0, rows)], sems.at[0]),
            pltpu.make_async_copy(second, left.at[pl.ds(rows, rows)], sems.at[1]),
        ]
        for n in range(parts):
            columns = pl.ds(n * step, step)
            todo.append(pltpu.make_async_copy(matrix.at[:, columns], right.at[:, columns], sems.at[2 + n]))
        return todo

    @pl.when(mine)
    def _():
        for copy in copies(ul_got, ul, ur):
            copy.start()

    @pl.when(jnp.logical_not(mine))
    def _():
        for copy in copies(dl, dl_got, dr):
            copy.start()

    waits = copies(ul, ul, ur)
    group = LANES // states_here
    live_states = states_ref[0]
    lane = iota((1, LANES), 1)
    live = (iota((states_here, LANES), 0) < live_states) & (
        iota((states_here, LANES), 1) % states_here < live_states
    )
    waits[0].wait()
    waits[1].wait()
    for n in range(parts):
        waits[2 + n].wait()
        full = jnp.dot(left[...], right[:, n * step : (n + 1) * step], preferred_element_type=F32)
        for p in range(0, 2 * rows, LANES):
            for q in range(0, step, LANES):
                block = full[p : p + LANES, q : q + LANES]
                distance = 1
                while distance < group:
                    four = block.reshape(group // (2 * distance), 2, distance * states_here, LANES)
                    size = group // 2 * states_here
                    low = four[:, 0].reshape(size, LANES)
                    high = four[:, 1].reshape(size, LANES)
                    odd = (lane // states_here // distance) % 2 == 1
                    shift = distance * states_here
                    new_low = jnp.where(odd, pltpu.roll(high, shift, 1), low)
                    new_high = jnp.where(odd, high, pltpu.roll(low, LANES - shift, 1))
                    shape = (group // (2 * distance), 1, distance * states_here, LANES)
                    block = jnp.concatenate([new_low.reshape(shape), new_high.reshape(shape)], axis=1)
                    block = block.reshape(LANES, LANES)
                    distance *= 2
                three = jnp.where(live[None], block.reshape(group, states_here, LANES), 0.0)
                out_ref[n * step + q : n * step + q + LANES, p : p + LANES] = three.reshape(
                    LANES, LANES
                ).astype(BF16)


def apply_kernel(*refs):
    *factors, half_ref, out_ref = refs
    chips = len(factors)
    chip = lax.axis_index("row") // 2
    depth = factors[0].shape[1]
    total = jnp.zeros(out_ref.shape, F32)
    for away in range(chips):
        source = lax.rem(chip - away + chips, chips)
        part = half_ref[pl.ds(pl.multiple_of(source * depth, depth), depth), :]
        total += jnp.dot(factors[away][...], part, preferred_element_type=F32)
    out_ref[...] = total.astype(BF16)


def finish_kernel(kept_ref, singular_ref, *refs, width):
    *parts, tilde_ref, proj_ref, inter_ref = refs
    chips = len(parts) // 2
    mine, got = parts[:chips], parts[chips:]
    keep_cols, rows = tilde_ref.shape
    core = lax.axis_index("row") % 2
    chip = lax.axis_index("row") // 2
    upper = is_upper()
    column = iota((1, keep_cols), 1)
    weight = jnp.where(column < kept_ref[0], 1.0 / jnp.sqrt(singular_ref[...]), 0.0)
    square = (keep_cols, keep_cols)
    diagonal = iota(square, 0) == iota(square, 1)
    weight_rows = jnp.sum(jnp.where(diagonal, weight, 0.0), axis=1, keepdims=True)
    products = []
    for away in range(chips):
        a = jnp.where(upper, mine[away][...], got[away][...])
        b = jnp.where(upper, got[away][...], mine[away][...])
        if away == 0:
            for whole, ref in ((a, tilde_ref), (b, proj_ref)):
                own = jnp.where(core == 0, whole[:, :rows], whole[:, rows:])
                ref[...] = (own.astype(F32) * weight_rows).astype(BF16)
        products.append(lax.dot_general(a, b, (((1,), (1,)), ((), ())), preferred_element_type=F32))
    total = jnp.zeros(square, F32)
    for source in range(chips):
        for away in range(chips):
            here = lax.rem(chip - away + chips, chips) == source
            total += jnp.where(here, products[away], 0.0)
    inter_ref[...] = total * weight_rows * weight / jnp.sqrt(jnp.float32(width))


def in_vmem():
    return pl.BlockSpec(memory_space=pltpu.VMEM)


def in_smem():
    return pl.BlockSpec(memory_space=pltpu.SMEM)


def local(
    sectors,
    row_devices,
    corner_ul,
    corner_ur,
    corner_dl,
    corner_dr,
    left_factor,
    right_factor,
    singular,
    states,
    kept,
    joining_map,
):
    rows, width = corner_ul.shape[1:]
    states_here = joining_map.shape[1]
    keep_cols = left_factor.shape[2]
    chips = row_devices // 2

    def other_core(value):
        return lax.ppermute(value, "row", [(i, i ^ 1) for i in range(row_devices)])

    def to_sector(value, upper_step, away):
        pairs = []
        for s in range(sectors):
            for r in range(row_devices):
                t = (s + (upper_step if r % 2 else -upper_step)) % sectors
                pairs.append((s * row_devices + r, t * row_devices + (r + 2 * away) % row_devices))
        return lax.ppermute(value, ("sec", "row"), pairs)

    u, v = left_factor[0].T, right_factor[0].T
    u_got, v_got = other_core(u), other_core(v)
    ul, dl = corner_ul[0], corner_dl[0]
    ul_got, dl_got = other_core(ul), other_core(dl)

    ordered = pl.pallas_call(
        order_kernel,
        out_shape=jax.ShapeDtypeStruct((keep_cols, 2 * rows), BF16),
        in_specs=[in_smem()] + [in_vmem()] * 4,
        out_specs=in_vmem(),
        name="order_factor",
    )(joining_map, u, u_got, v, v_got)
    factors = [to_sector(ordered, -1, away) for away in range(chips)]

    parts = width // (2 * LANES)
    anywhere = pl.BlockSpec(memory_space=pl.ANY)
    half = pl.pallas_call(
        functools.partial(half_kernel, parts=parts, states_here=states_here),
        out_shape=jax.ShapeDtypeStruct((width, 2 * rows), BF16),
        in_specs=[in_smem()] + [anywhere] * 6,
        out_specs=in_vmem(),
        scratch_shapes=[
            pltpu.VMEM((2 * rows, width), BF16),
            pltpu.VMEM((width, width), BF16),
            pltpu.SemaphoreType.DMA((2 + parts,)),
        ],
        compiler_params=pltpu.CompilerParams(vmem_limit_bytes=VMEM_BYTES),
        cost_estimate=pl.CostEstimate(
            flops=4 * rows * width * width, bytes_accessed=2 * width * (width + 4 * rows), transcendentals=0
        ),
        name="half_product",
    )(states, ul, ul_got, corner_ur[0], dl, dl_got, corner_dr[0])

    applied = pl.pallas_call(
        apply_kernel,
        out_shape=jax.ShapeDtypeStruct((keep_cols, 2 * rows), BF16),
        in_specs=[in_vmem()] * (chips + 1),
        out_specs=in_vmem(),
        compiler_params=pltpu.CompilerParams(vmem_limit_bytes=VMEM_BYTES),
        name="apply_factor",
    )(*factors, half)
    mine = [to_sector(applied, 1, away) for away in range(chips)]
    got = [other_core(value) for value in mine]

    tilde, proj, inter = pl.pallas_call(
        functools.partial(finish_kernel, width=width),
        out_shape=(
            jax.ShapeDtypeStruct((keep_cols, rows), BF16),
            jax.ShapeDtypeStruct((keep_cols, rows), BF16),
            jax.ShapeDtypeStruct((keep_cols, keep_cols), F32),
        ),
        in_specs=[in_smem()] + [in_vmem()] * (2 * chips + 1),
        out_specs=(in_vmem(), in_vmem(), in_vmem()),
        name="finish",
    )(kept, singular, *mine, *got)
    return tilde.T[None], proj.T[None], inter[None]


def solution(mesh):
    placed = (
        P("sec", "row", None),
        P("sec", None, None),
        P("sec", "row", None),
        P("sec", None, None),
        P("sec", "row", None),
        P("sec", "row", None),
        P("sec", None),
        P("sec"),
        P("sec"),
        P("sec", None),
    )
    return jax.shard_map(
        functools.partial(local, mesh.shape["sec"], mesh.shape["row"]),
        mesh=mesh,
        in_specs=placed,
        out_specs=(P("sec", "row", None), P("sec", "row", None), P("sec", None, None)),
        check_vma=False,
    )
```

```python
import functools

import jax
import jax.numpy as jnp
from jax import lax
from jax.experimental import pallas as pl
from jax.experimental.pallas import tpu as pltpu
from jax.sharding import PartitionSpec as P

LANES = 128
F32, BF16 = jnp.float32, jnp.bfloat16
MIB = 1024 * 1024
JOIN_FLOPS = 10**10


def iota(shape, dim):
    return lax.broadcasted_iota(jnp.int32, shape, dim)


def is_upper():
    return lax.axis_index("row") % 2 == 1


def join_kernel(own_ref, u_got_ref, v_got_ref, out_ref, *, states_here):
    keep_cols, rows = u_got_ref.shape
    upper = is_upper()
    own = own_ref[:keep_cols, :rows]
    got = jnp.where(upper, u_got_ref[...], v_got_ref[...])
    both = jnp.concatenate([jnp.where(upper, got, own), jnp.where(upper, own, got)], axis=1)
    lane = iota((1, LANES), 1)
    order = own_ref[keep_cols : keep_cols + 1, :LANES].astype(F32)
    order = jnp.where(lane < states_here, order, 0.0)
    distance = states_here
    while distance < LANES:
        order += pltpu.roll(order, distance, 1)
        distance *= 2
    wanted = order.astype(jnp.int32) + lane // states_here * states_here
    mover = jnp.where(iota((LANES, LANES), 0) == wanted, 1.0, 0.0).astype(BF16)
    for start in range(0, 2 * rows, LANES):
        moved = lax.dot_general(
            both[:, start : start + LANES], mover, (((1,), (1,)), ((), ())), preferred_element_type=F32
        )
        out_ref[:, start : start + LANES] = moved.astype(BF16)


def half_kernel(ul, ul_got, ur, dl, dl_got, dr, out_ref, *, states_here):
    rows, width = ul.shape
    step = 2 * LANES
    group = LANES // states_here
    lane = iota((1, LANES), 1)
    odd = {distance: (lane // states_here // distance) % 2 == 1 for distance in range(1, group)}

    def regroup(block):
        chunks = [block[i * states_here : (i + 1) * states_here] for i in range(group)]
        distance = 1
        while distance < group:
            shift = distance * states_here
            moved = list(chunks)
            for i in range(group):
                if i & distance == 0:
                    low, high = chunks[i], chunks[i + distance]
                    moved[i] = jnp.where(odd[distance], pltpu.roll(high, shift, 1), low)
                    moved[i + distance] = jnp.where(odd[distance], high, pltpu.roll(low, LANES - shift, 1))
            chunks = moved
            distance *= 2
        return chunks

    def work(first, second, matrix):
        if rows % LANES:
            lefts = [(0, jnp.concatenate([first[...], second[...]], axis=0))]
        else:
            lefts = [(0, first[...]), (rows, second[...])]
        for column in range(0, width, step):
            for base, left in lefts:
                full = jnp.dot(left, matrix[:, column : column + step], preferred_element_type=F32)
                for p in range(0, left.shape[0], LANES):
                    for q in range(0, step, LANES):
                        for i, chunk in enumerate(regroup(full[p : p + LANES, q : q + LANES])):
                            at = column + q + i * states_here
                            out_ref[at : at + states_here, base + p : base + p + LANES] = chunk.astype(BF16)

    upper = is_upper()

    @pl.when(upper)
    def _():
        work(ul_got, ul, ur)

    @pl.when(jnp.logical_not(upper))
    def _():
        work(dl, dl_got, dr)


def apply_kernel(states_ref, *refs, states_here):
    *factors, half_ref, out_ref = refs
    chips = len(factors)
    chip = lax.axis_index("row") // 2
    depth = factors[0].shape[1]
    live = iota((1, depth), 1) % states_here < states_ref[...]
    total = jnp.zeros(out_ref.shape, F32)
    for away in range(chips):
        source = lax.rem(chip - away + chips, chips)
        part = half_ref[pl.ds(pl.multiple_of(source * depth, depth), depth), :]
        factor = jnp.where(live, factors[away][...], jnp.zeros((), BF16))
        total += jnp.dot(factor, part, preferred_element_type=F32)
    out_ref[...] = jnp.where(live, total, 0.0).astype(BF16)


def finish_kernel(weight_ref, *refs, width):
    *parts, tilde_ref, proj_ref, inter_ref = refs
    chips = len(parts) // 2
    mine, got = parts[:chips], parts[chips:]
    keep_cols, rows = tilde_ref.shape
    core = lax.axis_index("row") % 2
    chip = lax.axis_index("row") // 2
    upper = is_upper()
    weight = weight_ref[...]
    square = (keep_cols, keep_cols)
    diagonal = iota(square, 0) == iota(square, 1)
    weight_rows = jnp.sum(jnp.where(diagonal, weight, 0.0), axis=1, keepdims=True)
    products = []
    for away in range(chips):
        a = jnp.where(upper, mine[away][...], got[away][...])
        b = jnp.where(upper, got[away][...], mine[away][...])
        if away == 0:
            for whole, ref in ((a, tilde_ref), (b, proj_ref)):
                own = jnp.where(core == 0, whole[:, :rows], whole[:, rows:])
                ref[...] = (own.astype(F32) * weight_rows).astype(BF16)
        products.append(lax.dot_general(a, b, (((1,), (1,)), ((), ())), preferred_element_type=F32))
    total = jnp.zeros(square, F32)
    for source in range(chips):
        for away in range(chips):
            here = lax.rem(chip - away + chips, chips) == source
            total += jnp.where(here, products[away], 0.0)
    inter_ref[...] = total * weight_rows * weight / jnp.sqrt(jnp.float32(width))


def in_vmem():
    return pl.BlockSpec(memory_space=pltpu.VMEM)


def local(
    sectors,
    row_devices,
    corner_ul,
    corner_ur,
    corner_dl,
    corner_dr,
    left_factor,
    right_factor,
    singular,
    states,
    kept,
    joining_map,
):
    rows, width = corner_ul.shape[1:]
    states_here = joining_map.shape[1]
    keep_cols = left_factor.shape[2]
    chips = row_devices // 2

    def other_core(value):
        return lax.ppermute(value, "row", [(i, i ^ 1) for i in range(row_devices)])

    def to_sector(value, upper_step, away):
        pairs = []
        for s in range(sectors):
            for r in range(row_devices):
                t = (s + (upper_step if r % 2 else -upper_step)) % sectors
                pairs.append((s * row_devices + r, t * row_devices + (r + 2 * away) % row_devices))
        return lax.ppermute(value, ("sec", "row"), pairs)

    block = jax.ShapeDtypeStruct((keep_cols, rows), BF16)
    whole = jax.ShapeDtypeStruct((keep_cols, 2 * rows), BF16)
    u, v = left_factor[0].T, right_factor[0].T
    u_got, v_got = other_core(u), other_core(v)
    own = jnp.where(is_upper(), u, v)
    own_width = max(rows, LANES)
    own = jnp.concatenate(
        [
            jnp.pad(own, ((0, 0), (0, own_width - rows))),
            jnp.pad(joining_map.astype(BF16), ((0, keep_cols - 1), (0, own_width - states_here))),
        ],
        axis=0,
    )
    joined = pl.pallas_call(
        functools.partial(join_kernel, states_here=states_here),
        out_shape=whole,
        in_specs=[in_vmem()] * 3,
        out_specs=in_vmem(),
        compiler_params=pltpu.CompilerParams(vmem_limit_bytes=MIB),
        cost_estimate=pl.CostEstimate(flops=JOIN_FLOPS, bytes_accessed=0, transcendentals=0),
        name="join_factor",
    )(own, u_got, v_got)
    factors = [to_sector(joined, -1, away) for away in range(chips)]

    ul, dl = corner_ul[0], corner_dl[0]
    ul_got, dl_got = other_core(ul), other_core(dl)
    half = pl.pallas_call(
        functools.partial(half_kernel, states_here=states_here),
        out_shape=jax.ShapeDtypeStruct((width, 2 * rows), BF16),
        in_specs=[in_vmem()] * 6,
        out_specs=in_vmem(),
        compiler_params=pltpu.CompilerParams(vmem_limit_bytes=16 * MIB),
        cost_estimate=pl.CostEstimate(
            flops=4 * rows * width * width, bytes_accessed=2 * width * (width + 4 * rows), transcendentals=0
        ),
        name="half_product",
    )(ul, ul_got, corner_ur[0], dl, dl_got, corner_dr[0])

    applied = pl.pallas_call(
        functools.partial(apply_kernel, states_here=states_here),
        out_shape=whole,
        in_specs=[in_vmem()] * (chips + 2),
        out_specs=in_vmem(),
        compiler_params=pltpu.CompilerParams(vmem_limit_bytes=4 * MIB),
        name="apply_factor",
    )(states[None], *factors, half)
    mine = [to_sector(applied, 1, away) for away in range(chips)]
    theirs = [other_core(value) for value in mine]

    columns = jnp.arange(keep_cols, dtype=jnp.int32)
    weight = jnp.where(columns < kept[0], 1.0 / jnp.sqrt(singular), 0.0)
    tilde, proj, inter = pl.pallas_call(
        functools.partial(finish_kernel, width=width),
        out_shape=(block, block, jax.ShapeDtypeStruct((keep_cols, keep_cols), F32)),
        in_specs=[in_vmem()] * (2 * chips + 1),
        out_specs=(in_vmem(), in_vmem(), in_vmem()),
        compiler_params=pltpu.CompilerParams(vmem_limit_bytes=MIB),
        name="finish",
    )(weight, *mine, *theirs)
    return tilde.T[None], proj.T[None], inter[None]


def solution(mesh):
    placed = (
        P("sec", "row", None),
        P("sec", None, None),
        P("sec", "row", None),
        P("sec", None, None),
        P("sec", "row", None),
        P("sec", "row", None),
        P("sec", None),
        P("sec"),
        P("sec"),
        P("sec", None),
    )
    return jax.shard_map(
        functools.partial(local, mesh.shape["sec"], mesh.shape["row"]),
        mesh=mesh,
        in_specs=placed,
        out_specs=(P("sec", "row", None), P("sec", "row", None), P("sec", None, None)),
        check_vma=False,
    )
```

```python
import functools

import jax
import jax.numpy as jnp
from jax import lax
from jax.experimental import pallas as pl
from jax.experimental.pallas import tpu as pltpu
from jax.sharding import PartitionSpec as P

LANES = 128
F32, BF16 = jnp.float32, jnp.bfloat16
MIB = 1024 * 1024
JOIN_FLOPS = 10**10
FACTOR_FIRST = (1, 1)
RESULT_FIRST = (1, 1)


def iota(shape, dim):
    return lax.broadcasted_iota(jnp.int32, shape, dim)


def is_upper():
    return lax.axis_index("row") & 1 == 1


def join_kernel(own_ref, u_got_ref, v_got_ref, out_ref, *, states_here):
    keep_cols, rows = u_got_ref.shape
    upper = is_upper()
    own = own_ref[:keep_cols, :rows].astype(BF16)
    got = jnp.where(upper, u_got_ref[...], v_got_ref[...])
    both = jnp.concatenate([jnp.where(upper, got, own), jnp.where(upper, own, got)], axis=1)
    lane = iota((1, LANES), 1)
    order = own_ref[keep_cols : keep_cols + 1, :LANES]
    order = jnp.where(lane < states_here, order, 0.0)
    distance = states_here
    while distance < LANES:
        order += pltpu.roll(order, distance, 1)
        distance *= 2
    wanted = order.astype(jnp.int32) + lane // states_here * states_here
    mover = jnp.where(iota((LANES, LANES), 0) == wanted, 1.0, 0.0).astype(BF16)
    for start in range(0, 2 * rows, LANES):
        moved = lax.dot_general(
            both[:, start : start + LANES], mover, (((1,), (1,)), ((), ())), preferred_element_type=F32
        )
        out_ref[:, start : start + LANES] = moved.astype(BF16)


def half_kernel(ul, ul_got, ur, dl, dl_got, dr, out_ref, *, states_here):
    rows, width = ul.shape
    step = 2 * LANES
    group = LANES // states_here
    lane = iota((1, LANES), 1)
    odd = {distance: (lane // states_here // distance) % 2 == 1 for distance in range(1, group)}

    def regroup(block):
        chunks = [block[i * states_here : (i + 1) * states_here] for i in range(group)]
        distance = 1
        while distance < group:
            shift = distance * states_here
            moved = list(chunks)
            for i in range(group):
                if i & distance == 0:
                    low, high = chunks[i], chunks[i + distance]
                    moved[i] = jnp.where(odd[distance], pltpu.roll(high, shift, 1), low)
                    moved[i + distance] = jnp.where(odd[distance], high, pltpu.roll(low, LANES - shift, 1))
            chunks = moved
            distance *= 2
        return chunks

    def work(first, second, matrix):
        if rows % LANES:
            lefts = [(0, jnp.concatenate([first[...], second[...]], axis=0))]
        else:
            lefts = [(0, first[...]), (rows, second[...])]
        for column in range(0, width, step):
            for base, left in lefts:
                full = jnp.dot(left, matrix[:, column : column + step], preferred_element_type=F32)
                for p in range(0, left.shape[0], LANES):
                    for q in range(0, step, LANES):
                        for i, chunk in enumerate(regroup(full[p : p + LANES, q : q + LANES])):
                            at = column + q + i * states_here
                            out_ref[at : at + states_here, base + p : base + p + LANES] = chunk.astype(BF16)

    upper = is_upper()

    @pl.when(upper)
    def _():
        work(ul_got, ul, ur)

    @pl.when(jnp.logical_not(upper))
    def _():
        work(dl, dl_got, dr)


def apply_kernel(states_ref, *refs, states_here):
    *factors, half_ref, out_ref = refs
    chips = len(factors)
    chip = lax.axis_index("row") // 2
    depth = factors[0].shape[1]
    live = iota((1, depth), 1) % states_here < states_ref[...]
    total = jnp.zeros(out_ref.shape, F32)
    first = jnp.where(is_upper(), FACTOR_FIRST[1], FACTOR_FIRST[0])
    for turn in range(chips):
        source = lax.rem(chip - turn - first + 2 * chips, chips)
        part = half_ref[pl.ds(pl.multiple_of(source * depth, depth), depth), :]
        factor = jnp.where(live, factors[turn][...], jnp.zeros((), BF16))
        total += jnp.dot(factor, part, preferred_element_type=F32)
    out_ref[...] = jnp.where(live, total, 0.0).astype(BF16)


def finish_kernel(weight_ref, *refs, width):
    *parts, tilde_ref, proj_ref, inter_ref = refs
    chips = len(parts) // 2
    mine, got = parts[:chips], parts[chips:]
    keep_cols, rows = tilde_ref.shape
    core = lax.axis_index("row") % 2
    chip = lax.axis_index("row") // 2
    upper = is_upper()
    weight = weight_ref[...]
    square = (keep_cols, keep_cols)
    diagonal = iota(square, 0) == iota(square, 1)
    weight_rows = jnp.sum(jnp.where(diagonal, weight, 0.0), axis=1, keepdims=True)
    lower_parts = [jnp.where(upper, got[turn][...], mine[turn][...]) for turn in range(chips)]
    upper_parts = [jnp.where(upper, mine[turn][...], got[turn][...]) for turn in range(chips)]
    lower_parts = [lower_parts[(away - RESULT_FIRST[0]) % chips] for away in range(chips)]
    upper_parts = [upper_parts[(away - RESULT_FIRST[1]) % chips] for away in range(chips)]
    for whole, ref in ((upper_parts[0], tilde_ref), (lower_parts[0], proj_ref)):
        own = jnp.where(core == 0, whole[:, :rows], whole[:, rows:])
        ref[...] = (own.astype(F32) * weight_rows).astype(BF16)
    products = [
        lax.dot_general(a, b, (((1,), (1,)), ((), ())), preferred_element_type=F32)
        for a, b in zip(upper_parts, lower_parts)
    ]
    total = jnp.zeros(square, F32)
    for source in range(chips):
        for away in range(chips):
            here = lax.rem(chip - away + chips, chips) == source
            total += jnp.where(here, products[away], 0.0)
    inter_ref[...] = total * weight_rows * weight / jnp.sqrt(jnp.float32(width))


def in_vmem():
    return pl.BlockSpec(memory_space=pltpu.VMEM)


def local(
    sectors,
    row_devices,
    corner_ul,
    corner_ur,
    corner_dl,
    corner_dr,
    left_factor,
    right_factor,
    singular,
    states,
    kept,
    joining_map,
):
    rows, width = corner_ul.shape[1:]
    states_here = joining_map.shape[1]
    keep_cols = left_factor.shape[2]
    chips = row_devices // 2

    def other_core(value):
        return lax.ppermute(value, "row", [(i, i ^ 1) for i in range(row_devices)])

    def to_sector(value, upper_step, turn, first):
        pairs = []
        for s in range(sectors):
            for r in range(row_devices):
                t = (s + (upper_step if r % 2 else -upper_step)) % sectors
                away = (turn + first[r % 2]) % chips
                pairs.append((s * row_devices + r, t * row_devices + (r + 2 * away) % row_devices))
        return lax.ppermute(value, ("sec", "row"), pairs)

    block = jax.ShapeDtypeStruct((keep_cols, rows), BF16)
    whole = jax.ShapeDtypeStruct((keep_cols, 2 * rows), BF16)
    u, v = left_factor[0].T, right_factor[0].T
    u_got, v_got = other_core(u), other_core(v)
    own_shape = (2 * keep_cols, max(rows, LANES))

    def placed(value, row):
        height, across = value.shape
        spare = (row, own_shape[0] - row - height, 0), (0, own_shape[1] - across, 0)
        return lax.pad(value, jnp.zeros((), value.dtype), spare)

    own = jnp.where(is_upper(), placed(u, 0), placed(v, 0)).astype(F32)
    own = jnp.where(iota(own_shape, 0) < keep_cols, own, placed(joining_map, keep_cols).astype(F32))
    joined = pl.pallas_call(
        functools.partial(join_kernel, states_here=states_here),
        out_shape=whole,
        in_specs=[in_vmem()] * 3,
        out_specs=in_vmem(),
        compiler_params=pltpu.CompilerParams(vmem_limit_bytes=MIB),
        cost_estimate=pl.CostEstimate(flops=JOIN_FLOPS, bytes_accessed=0, transcendentals=0),
        name="join_factor",
    )(own, u_got, v_got)
    factors = [to_sector(joined, -1, turn, FACTOR_FIRST) for turn in range(chips)]

    ul, dl = corner_ul[0], corner_dl[0]
    ul_later, dl_later, _ = lax.optimization_barrier((ul, dl, own))
    ul_got, dl_got = other_core(ul_later), other_core(dl_later)
    half = pl.pallas_call(
        functools.partial(half_kernel, states_here=states_here),
        out_shape=jax.ShapeDtypeStruct((width, 2 * rows), BF16),
        in_specs=[in_vmem()] * 6,
        out_specs=in_vmem(),
        compiler_params=pltpu.CompilerParams(vmem_limit_bytes=16 * MIB),
        cost_estimate=pl.CostEstimate(
            flops=rows * width, bytes_accessed=rows, transcendentals=0
        ),
        name="half_product",
    )(ul, ul_got, corner_ur[0], dl, dl_got, corner_dr[0])

    applied = pl.pallas_call(
        functools.partial(apply_kernel, states_here=states_here),
        out_shape=whole,
        in_specs=[in_vmem()] * (chips + 2),
        out_specs=in_vmem(),
        compiler_params=pltpu.CompilerParams(vmem_limit_bytes=4 * MIB),
        name="apply_factor",
    )(states[None], *factors, half)
    mine = [to_sector(applied, 1, turn, RESULT_FIRST) for turn in range(chips)]
    theirs = [other_core(value) for value in mine]

    columns = jnp.arange(keep_cols, dtype=jnp.int32)
    weight = jnp.where(columns < kept[0], 1.0 / jnp.sqrt(singular), 0.0)
    tilde, proj, inter = pl.pallas_call(
        functools.partial(finish_kernel, width=width),
        out_shape=(block, block, jax.ShapeDtypeStruct((keep_cols, keep_cols), F32)),
        in_specs=[in_vmem()] * (2 * chips + 1),
        out_specs=(in_vmem(), in_vmem(), in_vmem()),
        compiler_params=pltpu.CompilerParams(vmem_limit_bytes=MIB),
        name="finish",
    )(weight, *mine, *theirs)
    return tilde.T[None], proj.T[None], inter[None]


def solution(mesh):
    placed = (
        P("sec", "row", None),
        P("sec", None, None),
        P("sec", "row", None),
        P("sec", None, None),
        P("sec", "row", None),
        P("sec", "row", None),
        P("sec", None),
        P("sec"),
        P("sec"),
        P("sec", None),
    )
    return jax.shard_map(
        functools.partial(local, mesh.shape["sec"], mesh.shape["row"]),
        mesh=mesh,
        in_specs=placed,
        out_specs=(P("sec", "row", None), P("sec", "row", None), P("sec", None, None)),
        check_vma=False,
    )
```

```python
import functools

import jax
import jax.numpy as jnp
from jax import lax
from jax.experimental import pallas as pl
from jax.experimental.pallas import tpu as pltpu
from jax.sharding import PartitionSpec as P

LANES = 128
F32, BF16 = jnp.float32, jnp.bfloat16
MIB = 1024 * 1024
JOIN_FLOPS = 10**10
FACTOR_FIRST = (1, 1)
RESULT_FIRST = (1, 1)


def iota(shape, dim):
    return lax.broadcasted_iota(jnp.int32, shape, dim)


def is_upper():
    return lax.axis_index("row") & 1 == 1


def join_kernel(own_ref, u_got_ref, v_got_ref, out_ref, *, states_here):
    keep_cols, rows = u_got_ref.shape
    upper = is_upper()
    own = own_ref[:keep_cols, :rows].astype(BF16)
    got = jnp.where(upper, u_got_ref[...], v_got_ref[...])
    both = jnp.concatenate([jnp.where(upper, got, own), jnp.where(upper, own, got)], axis=1)
    shape = (states_here, LANES)
    order = jnp.broadcast_to(own_ref[keep_cols : keep_cols + 1, :LANES], shape)
    order = jnp.sum(jnp.where(iota(shape, 0) == iota(shape, 1), order, 0.0), axis=1, keepdims=True)
    order = jnp.broadcast_to(order, shape).astype(jnp.int32)
    square = (LANES, LANES)
    wanted = jnp.concatenate([order] * (LANES // states_here), axis=0) + iota(square, 0) // states_here * states_here
    mover = jnp.where(iota(square, 1) == wanted, 1.0, 0.0).astype(BF16)
    starts = range(0, 2 * rows, LANES)
    stacked = jnp.concatenate([both[:, start : start + LANES] for start in starts], axis=0)
    moved = jnp.dot(stacked, mover, preferred_element_type=F32).astype(BF16)
    for i, start in enumerate(starts):
        out_ref[:, start : start + LANES] = moved[i * keep_cols : (i + 1) * keep_cols]


def half_kernel(states_ref, ul, ul_got, ur, dl, dl_got, dr, out_ref, *, states_here):
    rows, width = ul.shape
    step = 2 * LANES
    group = LANES // states_here
    lane = iota((1, LANES), 1)
    chunk_shape = (states_here, LANES)
    live_rows = iota(chunk_shape, 0) < states_ref[0]
    live = live_rows & (iota(chunk_shape, 1) % states_here < states_ref[0])
    odd = {distance: (lane // states_here // distance) % 2 == 1 for distance in range(1, group)}

    def regroup(block):
        chunks = [block[i * states_here : (i + 1) * states_here] for i in range(group)]
        distance = 1
        while distance < group:
            shift = distance * states_here
            moved = list(chunks)
            for i in range(group):
                if i & distance == 0:
                    low, high = chunks[i], chunks[i + distance]
                    moved[i] = jnp.where(odd[distance], pltpu.roll(high, shift, 1), low)
                    moved[i + distance] = jnp.where(odd[distance], high, pltpu.roll(low, LANES - shift, 1))
            chunks = moved
            distance *= 2
        return chunks

    def work(first, second, matrix):
        if rows % LANES:
            lefts = [(0, jnp.concatenate([first[...], second[...]], axis=0))]
        else:
            lefts = [(0, first[...]), (rows, second[...])]
        for column in range(0, width, step):
            for base, left in lefts:
                full = jnp.dot(left, matrix[:, column : column + step], preferred_element_type=F32)
                for p in range(0, left.shape[0], LANES):
                    for q in range(0, step, LANES):
                        for i, chunk in enumerate(regroup(full[p : p + LANES, q : q + LANES])):
                            at = column + q + i * states_here
                            chunk = jnp.where(live, chunk, 0.0).astype(BF16)
                            out_ref[at : at + states_here, base + p : base + p + LANES] = chunk

    upper = is_upper()

    @pl.when(upper)
    def _():
        work(ul_got, ul, ur)

    @pl.when(jnp.logical_not(upper))
    def _():
        work(dl, dl_got, dr)


def apply_kernel(*refs):
    *factors, half_ref, out_ref = refs
    chips = len(factors)
    chip = lax.axis_index("row") // 2
    depth = factors[0].shape[1]
    total = jnp.zeros(out_ref.shape, F32)
    first = jnp.where(is_upper(), FACTOR_FIRST[1], FACTOR_FIRST[0])
    for turn in range(chips):
        source = lax.rem(chip - turn - first + 2 * chips, chips)
        part = half_ref[pl.ds(pl.multiple_of(source * depth, depth), depth), :]
        total += jnp.dot(factors[turn][...], part, preferred_element_type=F32)
    out_ref[...] = total.astype(BF16)


def finish_kernel(weight_ref, *refs, width):
    *parts, tilde_ref, proj_ref, inter_ref = refs
    chips = len(parts) // 2
    mine, got = parts[:chips], parts[chips:]
    keep_cols, rows = tilde_ref.shape
    core = lax.axis_index("row") % 2
    chip = lax.axis_index("row") // 2
    upper = is_upper()
    weight = weight_ref[...]
    square = (keep_cols, keep_cols)
    diagonal = iota(square, 0) == iota(square, 1)
    weight_rows = jnp.sum(jnp.where(diagonal, weight, 0.0), axis=1, keepdims=True)
    lower_parts = [jnp.where(upper, got[turn][...], mine[turn][...]) for turn in range(chips)]
    upper_parts = [jnp.where(upper, mine[turn][...], got[turn][...]) for turn in range(chips)]
    lower_parts = [lower_parts[(away - RESULT_FIRST[0]) % chips] for away in range(chips)]
    upper_parts = [upper_parts[(away - RESULT_FIRST[1]) % chips] for away in range(chips)]
    for whole, ref in ((upper_parts[0], tilde_ref), (lower_parts[0], proj_ref)):
        own = jnp.where(core == 0, whole[:, :rows], whole[:, rows:])
        ref[...] = (own.astype(F32) * weight_rows).astype(BF16)
    products = [
        lax.dot_general(a, b, (((1,), (1,)), ((), ())), preferred_element_type=F32)
        for a, b in zip(upper_parts, lower_parts)
    ]
    total = jnp.zeros(square, F32)
    for source in range(chips):
        for away in range(chips):
            here = lax.rem(chip - away + chips, chips) == source
            total += jnp.where(here, products[away], 0.0)
    inter_ref[...] = total * weight_rows * weight / jnp.sqrt(jnp.float32(width))


def in_vmem():
    return pl.BlockSpec(memory_space=pltpu.VMEM)


def local(
    sectors,
    row_devices,
    corner_ul,
    corner_ur,
    corner_dl,
    corner_dr,
    left_factor,
    right_factor,
    singular,
    states,
    kept,
    joining_map,
):
    rows, width = corner_ul.shape[1:]
    states_here = joining_map.shape[1]
    keep_cols = left_factor.shape[2]
    chips = row_devices // 2

    def other_core(value):
        return lax.ppermute(value, "row", [(i, i ^ 1) for i in range(row_devices)])

    def to_sector(value, upper_step, turn, first):
        pairs = []
        for s in range(sectors):
            for r in range(row_devices):
                t = (s + (upper_step if r % 2 else -upper_step)) % sectors
                away = (turn + first[r % 2]) % chips
                pairs.append((s * row_devices + r, t * row_devices + (r + 2 * away) % row_devices))
        return lax.ppermute(value, ("sec", "row"), pairs)

    block = jax.ShapeDtypeStruct((keep_cols, rows), BF16)
    whole = jax.ShapeDtypeStruct((keep_cols, 2 * rows), BF16)
    u, v = left_factor[0].T, right_factor[0].T
    u_got, v_got = other_core(u), other_core(v)
    own_shape = (2 * keep_cols, max(rows, LANES))

    def placed(value, row):
        height, across = value.shape
        spare = (row, own_shape[0] - row - height, 0), (0, own_shape[1] - across, 0)
        return lax.pad(value, jnp.zeros((), value.dtype), spare)

    own = jnp.where(is_upper(), placed(u, 0), placed(v, 0)).astype(F32)
    own = jnp.where(iota(own_shape, 0) < keep_cols, own, placed(joining_map, keep_cols).astype(F32))
    joined = pl.pallas_call(
        functools.partial(join_kernel, states_here=states_here),
        out_shape=whole,
        in_specs=[in_vmem()] * 3,
        out_specs=in_vmem(),
        compiler_params=pltpu.CompilerParams(vmem_limit_bytes=MIB),
        cost_estimate=pl.CostEstimate(flops=JOIN_FLOPS, bytes_accessed=0, transcendentals=0),
        name="join_factor",
    )(own, u_got, v_got)
    factors = [to_sector(joined, -1, turn, FACTOR_FIRST) for turn in range(chips)]

    ul, dl = corner_ul[0], corner_dl[0]
    ul_later, dl_later, _ = lax.optimization_barrier((ul, dl, own))
    ul_got, dl_got = other_core(ul_later), other_core(dl_later)
    half = pl.pallas_call(
        functools.partial(half_kernel, states_here=states_here),
        out_shape=jax.ShapeDtypeStruct((width, 2 * rows), BF16),
        in_specs=[pl.BlockSpec(memory_space=pltpu.SMEM)] + [in_vmem()] * 6,
        out_specs=in_vmem(),
        compiler_params=pltpu.CompilerParams(vmem_limit_bytes=16 * MIB),
        cost_estimate=pl.CostEstimate(
            flops=rows * width, bytes_accessed=rows, transcendentals=0
        ),
        name="half_product",
    )(states, ul, ul_got, corner_ur[0], dl, dl_got, corner_dr[0])

    applied = pl.pallas_call(
        apply_kernel,
        out_shape=whole,
        in_specs=[in_vmem()] * (chips + 1),
        out_specs=in_vmem(),
        compiler_params=pltpu.CompilerParams(vmem_limit_bytes=4 * MIB),
        name="apply_factor",
    )(*factors, half)
    mine = [to_sector(applied, 1, turn, RESULT_FIRST) for turn in range(chips)]
    theirs = [other_core(value) for value in mine]

    columns = jnp.arange(keep_cols, dtype=jnp.int32)
    weight = jnp.where(columns < kept[0], 1.0 / jnp.sqrt(singular), 0.0)
    tilde, proj, inter = pl.pallas_call(
        functools.partial(finish_kernel, width=width),
        out_shape=(block, block, jax.ShapeDtypeStruct((keep_cols, keep_cols), F32)),
        in_specs=[in_vmem()] * (2 * chips + 1),
        out_specs=(in_vmem(), in_vmem(), in_vmem()),
        compiler_params=pltpu.CompilerParams(vmem_limit_bytes=MIB),
        name="finish",
    )(weight, *mine, *theirs)
    return tilde.T[None], proj.T[None], inter[None]


def solution(mesh):
    placed = (
        P("sec", "row", None),
        P("sec", None, None),
        P("sec", "row", None),
        P("sec", None, None),
        P("sec", "row", None),
        P("sec", "row", None),
        P("sec", None),
        P("sec"),
        P("sec"),
        P("sec", None),
    )
    return jax.shard_map(
        functools.partial(local, mesh.shape["sec"], mesh.shape["row"]),
        mesh=mesh,
        in_specs=placed,
        out_specs=(P("sec", "row", None), P("sec", "row", None), P("sec", None, None)),
        check_vma=False,
    )
```

```python
import functools

import jax
import jax.numpy as jnp
from jax import lax
from jax.experimental import pallas as pl
from jax.experimental.pallas import tpu as pltpu
from jax.sharding import PartitionSpec as P

LANES = 128
F32, BF16 = jnp.float32, jnp.bfloat16
MIB = 1024 * 1024
JOIN_FLOPS = 10**10
FACTOR_FIRST = (1, 1)
RESULT_FIRST = (1, 1)


def iota(shape, dim):
    return lax.broadcasted_iota(jnp.int32, shape, dim)


def is_upper():
    return lax.axis_index("row") & 1 == 1


def join_kernel(own_ref, u_got_ref, v_got_ref, out_ref, *, states_here):
    keep_cols, rows = u_got_ref.shape
    upper = is_upper()
    own = own_ref[:keep_cols, :rows].astype(BF16)
    got = jnp.where(upper, u_got_ref[...], v_got_ref[...])
    both = jnp.concatenate([jnp.where(upper, got, own), jnp.where(upper, own, got)], axis=1)
    shape = (states_here, LANES)
    order = jnp.broadcast_to(own_ref[keep_cols : keep_cols + 1, :LANES], shape)
    order = jnp.sum(jnp.where(iota(shape, 0) == iota(shape, 1), order, 0.0), axis=1, keepdims=True)
    order = jnp.broadcast_to(order, shape).astype(jnp.int32)
    square = (LANES, LANES)
    wanted = jnp.concatenate([order] * (LANES // states_here), axis=0) + iota(square, 0) // states_here * states_here
    mover = jnp.where(iota(square, 1) == wanted, 1.0, 0.0).astype(BF16)
    starts = range(0, 2 * rows, LANES)
    stacked = jnp.concatenate([both[:, start : start + LANES] for start in starts], axis=0)
    moved = jnp.dot(stacked, mover, preferred_element_type=F32).astype(BF16)
    for i, start in enumerate(starts):
        out_ref[:, start : start + LANES] = moved[i * keep_cols : (i + 1) * keep_cols]


def half_kernel(states_ref, ul, ul_got, ur, dl, dl_got, dr, out_ref, *, states_here):
    rows, width = ul.shape
    step = 2 * LANES
    group = LANES // states_here
    lane = iota((1, LANES), 1)
    chunk_shape = (states_here, LANES)
    live_rows = iota(chunk_shape, 0) < states_ref[0]
    live = live_rows & (iota(chunk_shape, 1) % states_here < states_ref[0])
    odd = {distance: (lane // states_here // distance) % 2 == 1 for distance in range(1, group)}

    def regroup(block):
        chunks = [block[i * states_here : (i + 1) * states_here] for i in range(group)]
        distance = 1
        while distance < group:
            shift = distance * states_here
            moved = list(chunks)
            for i in range(group):
                if i & distance == 0:
                    low, high = chunks[i], chunks[i + distance]
                    moved[i] = jnp.where(odd[distance], pltpu.roll(high, shift, 1), low)
                    moved[i + distance] = jnp.where(odd[distance], high, pltpu.roll(low, LANES - shift, 1))
            chunks = moved
            distance *= 2
        return chunks

    def work(first, second, matrix):
        if rows % LANES:
            lefts = [(0, jnp.concatenate([first[...], second[...]], axis=0))]
        else:
            lefts = [(0, first[...]), (rows, second[...])]
        for column in range(0, width, step):
            for base, left in lefts:
                full = jnp.dot(left, matrix[:, column : column + step], preferred_element_type=F32)
                for p in range(0, left.shape[0], LANES):
                    for q in range(0, step, LANES):
                        for i, chunk in enumerate(regroup(full[p : p + LANES, q : q + LANES])):
                            at = column + q + i * states_here
                            chunk = jnp.where(live, chunk, 0.0).astype(BF16)
                            out_ref[at : at + states_here, base + p : base + p + LANES] = chunk

    upper = is_upper()

    @pl.when(upper)
    def _():
        work(ul_got, ul, ur)

    @pl.when(jnp.logical_not(upper))
    def _():
        work(dl, dl_got, dr)


def apply_kernel(*refs):
    *factors, half_ref, out_ref = refs
    chips = len(factors)
    chip = lax.axis_index("row") // 2
    depth = factors[0].shape[1]
    total = jnp.zeros(out_ref.shape, F32)
    first = jnp.where(is_upper(), FACTOR_FIRST[1], FACTOR_FIRST[0])
    for turn in range(chips):
        source = lax.rem(chip - turn - first + 2 * chips, chips)
        part = half_ref[pl.ds(pl.multiple_of(source * depth, depth), depth), :]
        total += jnp.dot(factors[turn][...], part, preferred_element_type=F32)
    out_ref[...] = total.astype(BF16)


def finish_kernel(kept_ref, singular_ref, mine_ref, got_ref, tilde_ref, proj_ref, inter_ref, *, width, chips):
    keep_cols, rows = tilde_ref.shape
    core = lax.axis_index("row") % 2
    chip = lax.axis_index("row") // 2
    upper = is_upper()
    weight = jnp.where(iota((1, keep_cols), 1) < kept_ref[0], 1.0 / jnp.sqrt(singular_ref[...]), 0.0)
    square = (keep_cols, keep_cols)
    diagonal = iota(square, 0) == iota(square, 1)
    weight_rows = jnp.sum(jnp.where(diagonal, weight, 0.0), axis=1, keepdims=True)
    turns = [pl.ds(turn * keep_cols, keep_cols) for turn in range(chips)]
    lower_parts = [jnp.where(upper, got_ref[turn], mine_ref[turn]) for turn in turns]
    upper_parts = [jnp.where(upper, mine_ref[turn], got_ref[turn]) for turn in turns]
    lower_parts = [lower_parts[(away - RESULT_FIRST[0]) % chips] for away in range(chips)]
    upper_parts = [upper_parts[(away - RESULT_FIRST[1]) % chips] for away in range(chips)]
    for whole, ref in ((upper_parts[0], tilde_ref), (lower_parts[0], proj_ref)):
        own = jnp.where(core == 0, whole[:, :rows], whole[:, rows:])
        ref[...] = (own.astype(F32) * weight_rows).astype(BF16)
    products = [
        lax.dot_general(a, b, (((1,), (1,)), ((), ())), preferred_element_type=F32)
        for a, b in zip(upper_parts, lower_parts)
    ]
    total = jnp.zeros(square, F32)
    for source in range(chips):
        for away in range(chips):
            here = lax.rem(chip - away + chips, chips) == source
            total += jnp.where(here, products[away], 0.0)
    inter_ref[...] = total * weight_rows * weight / jnp.sqrt(jnp.float32(width))


def in_vmem():
    return pl.BlockSpec(memory_space=pltpu.VMEM)


def local(
    sectors,
    row_devices,
    corner_ul,
    corner_ur,
    corner_dl,
    corner_dr,
    left_factor,
    right_factor,
    singular,
    states,
    kept,
    joining_map,
):
    rows, width = corner_ul.shape[1:]
    states_here = joining_map.shape[1]
    keep_cols = left_factor.shape[2]
    chips = row_devices // 2

    def other_core(value):
        return lax.ppermute(value, "row", [(i, i ^ 1) for i in range(row_devices)])

    def to_sector(value, upper_step, turn, first):
        pairs = []
        for s in range(sectors):
            for r in range(row_devices):
                t = (s + (upper_step if r % 2 else -upper_step)) % sectors
                away = (turn + first[r % 2]) % chips
                pairs.append((s * row_devices + r, t * row_devices + (r + 2 * away) % row_devices))
        return lax.ppermute(value, ("sec", "row"), pairs)

    block = jax.ShapeDtypeStruct((keep_cols, rows), BF16)
    whole = jax.ShapeDtypeStruct((keep_cols, 2 * rows), BF16)
    u, v = left_factor[0].T, right_factor[0].T
    u_got, v_got = other_core(u), other_core(v)
    own_shape = (2 * keep_cols, max(rows, LANES))

    def placed(value, row):
        height, across = value.shape
        spare = (row, own_shape[0] - row - height, 0), (0, own_shape[1] - across, 0)
        return lax.pad(value, jnp.zeros((), value.dtype), spare)

    own = jnp.where(is_upper(), placed(u, 0), placed(v, 0)).astype(F32)
    own = jnp.where(iota(own_shape, 0) < keep_cols, own, placed(joining_map, keep_cols).astype(F32))
    joined = pl.pallas_call(
        functools.partial(join_kernel, states_here=states_here),
        out_shape=whole,
        in_specs=[in_vmem()] * 3,
        out_specs=in_vmem(),
        compiler_params=pltpu.CompilerParams(vmem_limit_bytes=MIB),
        cost_estimate=pl.CostEstimate(flops=JOIN_FLOPS, bytes_accessed=0, transcendentals=0),
        name="join_factor",
    )(own, u_got, v_got)
    factors = [to_sector(joined, -1, turn, FACTOR_FIRST) for turn in range(chips)]

    ul, dl = corner_ul[0], corner_dl[0]
    ul_later, dl_later, _ = lax.optimization_barrier((ul, dl, own))
    ul_got, dl_got = other_core(ul_later), other_core(dl_later)
    half = pl.pallas_call(
        functools.partial(half_kernel, states_here=states_here),
        out_shape=jax.ShapeDtypeStruct((width, 2 * rows), BF16),
        in_specs=[pl.BlockSpec(memory_space=pltpu.SMEM)] + [in_vmem()] * 6,
        out_specs=in_vmem(),
        compiler_params=pltpu.CompilerParams(vmem_limit_bytes=16 * MIB),
        cost_estimate=pl.CostEstimate(
            flops=rows * width, bytes_accessed=rows, transcendentals=0
        ),
        name="half_product",
    )(states, ul, ul_got, corner_ur[0], dl, dl_got, corner_dr[0])

    applied = pl.pallas_call(
        apply_kernel,
        out_shape=whole,
        in_specs=[in_vmem()] * (chips + 1),
        out_specs=in_vmem(),
        compiler_params=pltpu.CompilerParams(vmem_limit_bytes=4 * MIB),
        name="apply_factor",
    )(*factors, half)
    mine = [to_sector(applied, 1, turn, RESULT_FIRST) for turn in range(chips)]
    mine = jnp.concatenate(mine, axis=0)
    theirs = other_core(mine)

    tilde, proj, inter = pl.pallas_call(
        functools.partial(finish_kernel, width=width, chips=chips),
        out_shape=(block, block, jax.ShapeDtypeStruct((keep_cols, keep_cols), F32)),
        in_specs=[pl.BlockSpec(memory_space=pltpu.SMEM)] + [in_vmem()] * 3,
        out_specs=(in_vmem(), in_vmem(), in_vmem()),
        compiler_params=pltpu.CompilerParams(vmem_limit_bytes=MIB),
        name="finish",
    )(kept, singular, mine, theirs)
    return tilde.T[None], proj.T[None], inter[None]


def solution(mesh):
    placed = (
        P("sec", "row", None),
        P("sec", None, None),
        P("sec", "row", None),
        P("sec", None, None),
        P("sec", "row", None),
        P("sec", "row", None),
        P("sec", None),
        P("sec"),
        P("sec"),
        P("sec", None),
    )
    return jax.shard_map(
        functools.partial(local, mesh.shape["sec"], mesh.shape["row"]),
        mesh=mesh,
        in_specs=placed,
        out_specs=(P("sec", "row", None), P("sec", "row", None), P("sec", None, None)),
        check_vma=False,
    )
```

```python
import functools

import jax
import jax.numpy as jnp
from jax import lax
from jax.experimental import pallas as pl
from jax.experimental.pallas import tpu as pltpu
from jax.sharding import PartitionSpec as P

LANES = 128
F32, BF16 = jnp.float32, jnp.bfloat16
MIB = 1024 * 1024
START_FLOPS = 2 * 10**9
JOIN_FLOPS = 10**10
FACTOR_FIRST = (1, 1)
RESULT_FIRST = (1, 1)


def iota(shape, dim):
    return lax.broadcasted_iota(jnp.int32, shape, dim)


def is_upper():
    return lax.axis_index("row") & 1 == 1


def start_kernel(out_ref):
    out_ref[...] = jnp.zeros(out_ref.shape, F32)


def own_kernel(after_ref, map_ref, u_ref, v_ref, own_ref, mover_ref):
    states_here = map_ref.shape[1]
    own_ref[...] = jnp.where(is_upper(), u_ref[...], v_ref[...])
    small = (states_here, states_here)
    entries = jnp.where(iota(small, 0) == iota(small, 1), map_ref[...].astype(F32), 0.0)
    entries = jnp.sum(entries, axis=1, keepdims=True).astype(jnp.int32)
    entries = jnp.broadcast_to(entries, (states_here, LANES))
    square = (LANES, LANES)
    wanted = jnp.concatenate([entries] * (LANES // states_here), axis=0) + iota(square, 0) // states_here * states_here
    mover_ref[...] = jnp.where(iota(square, 1) == wanted, 1.0, 0.0).astype(BF16)


def join_kernel(own_ref, mover_ref, u_got_ref, v_got_ref, out_ref):
    keep_cols, rows = u_got_ref.shape
    upper = is_upper()
    own = own_ref[...]
    got = jnp.where(upper, u_got_ref[...], v_got_ref[...])
    both = jnp.concatenate([jnp.where(upper, got, own), jnp.where(upper, own, got)], axis=1)
    starts = range(0, 2 * rows, LANES)
    stacked = jnp.concatenate([both[:, start : start + LANES] for start in starts], axis=0)
    moved = jnp.dot(stacked, mover_ref[...], preferred_element_type=F32).astype(BF16)
    for i, start in enumerate(starts):
        out_ref[:, start : start + LANES] = moved[i * keep_cols : (i + 1) * keep_cols]


def half_kernel(states_ref, ul, ul_got, ur, dl, dl_got, dr, out_ref, *, states_here):
    rows, width = ul.shape
    step = 2 * LANES
    group = LANES // states_here
    lane = iota((1, LANES), 1)
    chunk_shape = (states_here, LANES)
    live_rows = iota(chunk_shape, 0) < states_ref[0]
    live = live_rows & (iota(chunk_shape, 1) % states_here < states_ref[0])
    odd = {distance: (lane // states_here // distance) % 2 == 1 for distance in range(1, group)}

    def regroup(block):
        chunks = [block[i * states_here : (i + 1) * states_here] for i in range(group)]
        distance = 1
        while distance < group:
            shift = distance * states_here
            moved = list(chunks)
            for i in range(group):
                if i & distance == 0:
                    low, high = chunks[i], chunks[i + distance]
                    moved[i] = jnp.where(odd[distance], pltpu.roll(high, shift, 1), low)
                    moved[i + distance] = jnp.where(odd[distance], high, pltpu.roll(low, LANES - shift, 1))
            chunks = moved
            distance *= 2
        return chunks

    def work(first, second, matrix):
        if rows % LANES:
            lefts = [(0, jnp.concatenate([first[...], second[...]], axis=0))]
        else:
            lefts = [(0, first[...]), (rows, second[...])]
        for column in range(0, width, step):
            for base, left in lefts:
                full = jnp.dot(left, matrix[:, column : column + step], preferred_element_type=F32)
                for p in range(0, left.shape[0], LANES):
                    for q in range(0, step, LANES):
                        for i, chunk in enumerate(regroup(full[p : p + LANES, q : q + LANES])):
                            at = column + q + i * states_here
                            chunk = jnp.where(live, chunk, 0.0).astype(BF16)
                            out_ref[at : at + states_here, base + p : base + p + LANES] = chunk

    upper = is_upper()

    @pl.when(upper)
    def _():
        work(ul_got, ul, ur)

    @pl.when(jnp.logical_not(upper))
    def _():
        work(dl, dl_got, dr)


def apply_kernel(*refs):
    *factors, half_ref, out_ref = refs
    chips = len(factors)
    chip = lax.axis_index("row") // 2
    depth = factors[0].shape[1]
    total = jnp.zeros(out_ref.shape, F32)
    first = jnp.where(is_upper(), FACTOR_FIRST[1], FACTOR_FIRST[0])
    for turn in range(chips):
        source = lax.rem(chip - turn - first + 2 * chips, chips)
        part = half_ref[pl.ds(pl.multiple_of(source * depth, depth), depth), :]
        total += jnp.dot(factors[turn][...], part, preferred_element_type=F32)
    out_ref[...] = total.astype(BF16)


def finish_kernel(kept_ref, singular_ref, mine_ref, got_ref, tilde_ref, proj_ref, inter_ref, *, width, chips):
    keep_cols, rows = tilde_ref.shape
    core = lax.axis_index("row") % 2
    chip = lax.axis_index("row") // 2
    upper = is_upper()
    weight = jnp.where(iota((1, keep_cols), 1) < kept_ref[0], 1.0 / jnp.sqrt(singular_ref[...]), 0.0)
    square = (keep_cols, keep_cols)
    diagonal = iota(square, 0) == iota(square, 1)
    weight_rows = jnp.sum(jnp.where(diagonal, weight, 0.0), axis=1, keepdims=True)
    turns = [pl.ds(turn * keep_cols, keep_cols) for turn in range(chips)]
    lower_parts = [jnp.where(upper, got_ref[turn], mine_ref[turn]) for turn in turns]
    upper_parts = [jnp.where(upper, mine_ref[turn], got_ref[turn]) for turn in turns]
    lower_parts = [lower_parts[(away - RESULT_FIRST[0]) % chips] for away in range(chips)]
    upper_parts = [upper_parts[(away - RESULT_FIRST[1]) % chips] for away in range(chips)]
    for whole, ref in ((upper_parts[0], tilde_ref), (lower_parts[0], proj_ref)):
        own = jnp.where(core == 0, whole[:, :rows], whole[:, rows:])
        ref[...] = (own.astype(F32) * weight_rows).astype(BF16)
    products = [
        lax.dot_general(a, b, (((1,), (1,)), ((), ())), preferred_element_type=F32)
        for a, b in zip(upper_parts, lower_parts)
    ]
    total = jnp.zeros(square, F32)
    for source in range(chips):
        for away in range(chips):
            here = lax.rem(chip - away + chips, chips) == source
            total += jnp.where(here, products[away], 0.0)
    inter_ref[...] = total * weight_rows * weight / jnp.sqrt(jnp.float32(width))


def in_vmem():
    return pl.BlockSpec(memory_space=pltpu.VMEM)


def local(
    sectors,
    row_devices,
    corner_ul,
    corner_ur,
    corner_dl,
    corner_dr,
    left_factor,
    right_factor,
    singular,
    states,
    kept,
    joining_map,
):
    rows, width = corner_ul.shape[1:]
    states_here = joining_map.shape[1]
    keep_cols = left_factor.shape[2]
    chips = row_devices // 2

    def other_core(value):
        return lax.ppermute(value, "row", [(i, i ^ 1) for i in range(row_devices)])

    def to_sector(value, upper_step, turn, first):
        pairs = []
        for s in range(sectors):
            for r in range(row_devices):
                t = (s + (upper_step if r % 2 else -upper_step)) % sectors
                away = (turn + first[r % 2]) % chips
                pairs.append((s * row_devices + r, t * row_devices + (r + 2 * away) % row_devices))
        return lax.ppermute(value, ("sec", "row"), pairs)

    block = jax.ShapeDtypeStruct((keep_cols, rows), BF16)
    whole = jax.ShapeDtypeStruct((keep_cols, 2 * rows), BF16)
    u, v = left_factor[0].T, right_factor[0].T
    u_got, v_got = other_core(u), other_core(v)
    waited = pl.pallas_call(
        start_kernel,
        out_shape=jax.ShapeDtypeStruct((8, LANES), F32),
        in_specs=[],
        out_specs=in_vmem(),
        compiler_params=pltpu.CompilerParams(vmem_limit_bytes=MIB),
        cost_estimate=pl.CostEstimate(flops=START_FLOPS, bytes_accessed=0, transcendentals=0),
        name="start",
    )()
    own, mover = pl.pallas_call(
        own_kernel,
        out_shape=(block, jax.ShapeDtypeStruct((LANES, LANES), BF16)),
        in_specs=[in_vmem()] * 4,
        out_specs=(in_vmem(), in_vmem()),
        compiler_params=pltpu.CompilerParams(vmem_limit_bytes=MIB),
        name="own_factor",
    )(waited, joining_map, u, v)
    joined = pl.pallas_call(
        join_kernel,
        out_shape=whole,
        in_specs=[in_vmem()] * 4,
        out_specs=in_vmem(),
        compiler_params=pltpu.CompilerParams(vmem_limit_bytes=MIB),
        cost_estimate=pl.CostEstimate(flops=JOIN_FLOPS, bytes_accessed=0, transcendentals=0),
        name="join_factor",
    )(own, mover, u_got, v_got)
    factors = [to_sector(joined, -1, turn, FACTOR_FIRST) for turn in range(chips)]

    ul, dl = corner_ul[0], corner_dl[0]
    ul_got, dl_got = other_core(ul), other_core(dl)
    half = pl.pallas_call(
        functools.partial(half_kernel, states_here=states_here),
        out_shape=jax.ShapeDtypeStruct((width, 2 * rows), BF16),
        in_specs=[pl.BlockSpec(memory_space=pltpu.SMEM)] + [in_vmem()] * 6,
        out_specs=in_vmem(),
        compiler_params=pltpu.CompilerParams(vmem_limit_bytes=16 * MIB),
        cost_estimate=pl.CostEstimate(
            flops=rows * width, bytes_accessed=rows, transcendentals=0
        ),
        name="half_product",
    )(states, ul, ul_got, corner_ur[0], dl, dl_got, corner_dr[0])

    applied = pl.pallas_call(
        apply_kernel,
        out_shape=whole,
        in_specs=[in_vmem()] * (chips + 1),
        out_specs=in_vmem(),
        compiler_params=pltpu.CompilerParams(vmem_limit_bytes=4 * MIB),
        name="apply_factor",
    )(*factors, half)
    mine = [to_sector(applied, 1, turn, RESULT_FIRST) for turn in range(chips)]
    mine = jnp.concatenate(mine, axis=0)
    theirs = other_core(mine)

    tilde, proj, inter = pl.pallas_call(
        functools.partial(finish_kernel, width=width, chips=chips),
        out_shape=(block, block, jax.ShapeDtypeStruct((keep_cols, keep_cols), F32)),
        in_specs=[pl.BlockSpec(memory_space=pltpu.SMEM)] + [in_vmem()] * 3,
        out_specs=(in_vmem(), in_vmem(), in_vmem()),
        compiler_params=pltpu.CompilerParams(vmem_limit_bytes=MIB),
        name="finish",
    )(kept, singular, mine, theirs)
    return tilde.T[None], proj.T[None], inter[None]


def solution(mesh):
    placed = (
        P("sec", "row", None),
        P("sec", None, None),
        P("sec", "row", None),
        P("sec", None, None),
        P("sec", "row", None),
        P("sec", "row", None),
        P("sec", None),
        P("sec"),
        P("sec"),
        P("sec", None),
    )
    return jax.shard_map(
        functools.partial(local, mesh.shape["sec"], mesh.shape["row"]),
        mesh=mesh,
        in_specs=placed,
        out_specs=(P("sec", "row", None), P("sec", "row", None), P("sec", None, None)),
        check_vma=False,
    )
```

```python
import functools

import jax
import jax.numpy as jnp
from jax import lax
from jax.experimental import pallas as pl
from jax.experimental.pallas import tpu as pltpu
from jax.sharding import PartitionSpec as P

LANES = 128
F32, BF16 = jnp.float32, jnp.bfloat16
MIB = 1024 * 1024
START_FLOPS = 2 * 10**9
JOIN_FLOPS = 10**10
FACTOR_FIRST = (1, 1)
RESULT_FIRST = (1, 1)
FACTOR_WRAP = (1, 0)
RESULT_WRAP = (1, 1)


def iota(shape, dim):
    return lax.broadcasted_iota(jnp.int32, shape, dim)


def is_upper():
    return lax.axis_index("row") & 1 == 1


def start_kernel(out_ref):
    out_ref[...] = jnp.zeros(out_ref.shape, F32)


def own_kernel(after_ref, map_ref, u_ref, v_ref, own_ref, mover_ref):
    states_here = map_ref.shape[1]
    own_ref[...] = jnp.where(is_upper(), u_ref[...], v_ref[...])
    small = (states_here, states_here)
    entries = jnp.where(iota(small, 0) == iota(small, 1), map_ref[...].astype(F32), 0.0)
    entries = jnp.sum(entries, axis=1, keepdims=True).astype(jnp.int32)
    entries = jnp.broadcast_to(entries, (states_here, LANES))
    square = (LANES, LANES)
    wanted = jnp.concatenate([entries] * (LANES // states_here), axis=0) + iota(square, 0) // states_here * states_here
    mover_ref[...] = jnp.where(iota(square, 1) == wanted, 1.0, 0.0).astype(BF16)


def join_kernel(own_ref, mover_ref, u_got_ref, v_got_ref, out_ref):
    keep_cols, rows = u_got_ref.shape
    upper = is_upper()
    own = own_ref[...]
    got = jnp.where(upper, u_got_ref[...], v_got_ref[...])
    both = jnp.concatenate([jnp.where(upper, got, own), jnp.where(upper, own, got)], axis=1)
    starts = range(0, 2 * rows, LANES)
    stacked = jnp.concatenate([both[:, start : start + LANES] for start in starts], axis=0)
    moved = jnp.dot(stacked, mover_ref[...], preferred_element_type=F32).astype(BF16)
    for i, start in enumerate(starts):
        out_ref[:, start : start + LANES] = moved[i * keep_cols : (i + 1) * keep_cols]


def half_kernel(states_ref, ul, ul_got, ur, dl, dl_got, dr, out_ref, *, states_here):
    rows, width = ul.shape
    step = 2 * LANES
    group = LANES // states_here
    lane = iota((1, LANES), 1)
    chunk_shape = (states_here, LANES)
    live_rows = iota(chunk_shape, 0) < states_ref[0]
    live = live_rows & (iota(chunk_shape, 1) % states_here < states_ref[0])
    odd = {distance: (lane // states_here // distance) % 2 == 1 for distance in range(1, group)}

    def regroup(block):
        chunks = [block[i * states_here : (i + 1) * states_here] for i in range(group)]
        distance = 1
        while distance < group:
            shift = distance * states_here
            moved = list(chunks)
            for i in range(group):
                if i & distance == 0:
                    low, high = chunks[i], chunks[i + distance]
                    moved[i] = jnp.where(odd[distance], pltpu.roll(high, shift, 1), low)
                    moved[i + distance] = jnp.where(odd[distance], high, pltpu.roll(low, LANES - shift, 1))
            chunks = moved
            distance *= 2
        return chunks

    def work(first, second, matrix):
        if rows % LANES:
            lefts = [(0, jnp.concatenate([first[...], second[...]], axis=0))]
        else:
            lefts = [(0, first[...]), (rows, second[...])]
        for column in range(0, width, step):
            for base, left in lefts:
                full = jnp.dot(left, matrix[:, column : column + step], preferred_element_type=F32)
                for p in range(0, left.shape[0], LANES):
                    for q in range(0, step, LANES):
                        for i, chunk in enumerate(regroup(full[p : p + LANES, q : q + LANES])):
                            at = column + q + i * states_here
                            chunk = jnp.where(live, chunk, 0.0).astype(BF16)
                            out_ref[at : at + states_here, base + p : base + p + LANES] = chunk

    upper = is_upper()

    @pl.when(upper)
    def _():
        work(ul_got, ul, ur)

    @pl.when(jnp.logical_not(upper))
    def _():
        work(dl, dl_got, dr)


def apply_kernel(*refs):
    *factors, half_ref, out_ref = refs
    chips = len(factors)
    chip = lax.axis_index("row") // 2
    depth = factors[0].shape[1]
    total = jnp.zeros(out_ref.shape, F32)
    sector, last = lax.axis_index("sec"), lax.axis_size("sec") - 1
    first = jnp.where(
        is_upper(),
        jnp.where(sector == last, FACTOR_WRAP[1], FACTOR_FIRST[1]),
        jnp.where(sector == 0, FACTOR_WRAP[0], FACTOR_FIRST[0]),
    )
    for turn in range(chips):
        source = lax.rem(chip - turn - first + 2 * chips, chips)
        part = half_ref[pl.ds(pl.multiple_of(source * depth, depth), depth), :]
        total += jnp.dot(factors[turn][...], part, preferred_element_type=F32)
    out_ref[...] = total.astype(BF16)


def finish_kernel(kept_ref, singular_ref, mine_ref, got_ref, tilde_ref, proj_ref, inter_ref, *, width, chips):
    keep_cols, rows = tilde_ref.shape
    core = lax.axis_index("row") % 2
    chip = lax.axis_index("row") // 2
    upper = is_upper()
    weight = jnp.where(iota((1, keep_cols), 1) < kept_ref[0], 1.0 / jnp.sqrt(singular_ref[...]), 0.0)
    square = (keep_cols, keep_cols)
    diagonal = iota(square, 0) == iota(square, 1)
    weight_rows = jnp.sum(jnp.where(diagonal, weight, 0.0), axis=1, keepdims=True)
    turns = [pl.ds(turn * keep_cols, keep_cols) for turn in range(chips)]
    lower_parts = [jnp.where(upper, got_ref[turn], mine_ref[turn]) for turn in turns]
    upper_parts = [jnp.where(upper, mine_ref[turn], got_ref[turn]) for turn in turns]
    sector, last = lax.axis_index("sec"), lax.axis_size("sec") - 1

    def ordered(parts, core, wraps):
        found = []
        for away in range(chips):
            usual = parts[(away - RESULT_FIRST[core]) % chips]
            wrapped = parts[(away - RESULT_WRAP[core]) % chips]
            found.append(jnp.where(wraps, wrapped, usual))
        return found

    lower_parts = ordered(lower_parts, 0, sector == last)
    upper_parts = ordered(upper_parts, 1, sector == 0)
    for whole, ref in ((upper_parts[0], tilde_ref), (lower_parts[0], proj_ref)):
        own = jnp.where(core == 0, whole[:, :rows], whole[:, rows:])
        ref[...] = (own.astype(F32) * weight_rows).astype(BF16)
    products = [
        lax.dot_general(a, b, (((1,), (1,)), ((), ())), preferred_element_type=F32)
        for a, b in zip(upper_parts, lower_parts)
    ]
    total = jnp.zeros(square, F32)
    for source in range(chips):
        for away in range(chips):
            here = lax.rem(chip - away + chips, chips) == source
            total += jnp.where(here, products[away], 0.0)
    inter_ref[...] = total * weight_rows * weight / jnp.sqrt(jnp.float32(width))


def in_vmem():
    return pl.BlockSpec(memory_space=pltpu.VMEM)


def local(
    sectors,
    row_devices,
    corner_ul,
    corner_ur,
    corner_dl,
    corner_dr,
    left_factor,
    right_factor,
    singular,
    states,
    kept,
    joining_map,
):
    rows, width = corner_ul.shape[1:]
    states_here = joining_map.shape[1]
    keep_cols = left_factor.shape[2]
    chips = row_devices // 2

    def other_core(value):
        return lax.ppermute(value, "row", [(i, i ^ 1) for i in range(row_devices)])

    def to_sector(value, upper_step, turn, first, wrap):
        pairs = []
        for s in range(sectors):
            for r in range(row_devices):
                t = s + (upper_step if r % 2 else -upper_step)
                away = (turn + (first if 0 <= t < sectors else wrap)[r % 2]) % chips
                pairs.append((s * row_devices + r, t % sectors * row_devices + (r + 2 * away) % row_devices))
        return lax.ppermute(value, ("sec", "row"), pairs)

    block = jax.ShapeDtypeStruct((keep_cols, rows), BF16)
    whole = jax.ShapeDtypeStruct((keep_cols, 2 * rows), BF16)
    u, v = left_factor[0].T, right_factor[0].T
    u_got, v_got = other_core(u), other_core(v)
    waited = pl.pallas_call(
        start_kernel,
        out_shape=jax.ShapeDtypeStruct((8, LANES), F32),
        in_specs=[],
        out_specs=in_vmem(),
        compiler_params=pltpu.CompilerParams(vmem_limit_bytes=MIB),
        cost_estimate=pl.CostEstimate(flops=START_FLOPS, bytes_accessed=0, transcendentals=0),
        name="start",
    )()
    own, mover = pl.pallas_call(
        own_kernel,
        out_shape=(block, jax.ShapeDtypeStruct((LANES, LANES), BF16)),
        in_specs=[in_vmem()] * 4,
        out_specs=(in_vmem(), in_vmem()),
        compiler_params=pltpu.CompilerParams(vmem_limit_bytes=MIB),
        name="own_factor",
    )(waited, joining_map, u, v)
    joined = pl.pallas_call(
        join_kernel,
        out_shape=whole,
        in_specs=[in_vmem()] * 4,
        out_specs=in_vmem(),
        compiler_params=pltpu.CompilerParams(vmem_limit_bytes=MIB),
        cost_estimate=pl.CostEstimate(flops=JOIN_FLOPS, bytes_accessed=0, transcendentals=0),
        name="join_factor",
    )(own, mover, u_got, v_got)
    factors = [to_sector(joined, -1, turn, FACTOR_FIRST, FACTOR_WRAP) for turn in range(chips)]

    ul, dl = corner_ul[0], corner_dl[0]
    ul_got, dl_got = other_core(ul), other_core(dl)
    half = pl.pallas_call(
        functools.partial(half_kernel, states_here=states_here),
        out_shape=jax.ShapeDtypeStruct((width, 2 * rows), BF16),
        in_specs=[pl.BlockSpec(memory_space=pltpu.SMEM)] + [in_vmem()] * 6,
        out_specs=in_vmem(),
        compiler_params=pltpu.CompilerParams(vmem_limit_bytes=16 * MIB),
        cost_estimate=pl.CostEstimate(
            flops=rows * width, bytes_accessed=rows, transcendentals=0
        ),
        name="half_product",
    )(states, ul, ul_got, corner_ur[0], dl, dl_got, corner_dr[0])

    applied = pl.pallas_call(
        apply_kernel,
        out_shape=whole,
        in_specs=[in_vmem()] * (chips + 1),
        out_specs=in_vmem(),
        compiler_params=pltpu.CompilerParams(vmem_limit_bytes=4 * MIB),
        name="apply_factor",
    )(*factors, half)
    mine = [to_sector(applied, 1, turn, RESULT_FIRST, RESULT_WRAP) for turn in range(chips)]
    mine = jnp.concatenate(mine, axis=0)
    theirs = other_core(mine)

    tilde, proj, inter = pl.pallas_call(
        functools.partial(finish_kernel, width=width, chips=chips),
        out_shape=(block, block, jax.ShapeDtypeStruct((keep_cols, keep_cols), F32)),
        in_specs=[pl.BlockSpec(memory_space=pltpu.SMEM)] + [in_vmem()] * 3,
        out_specs=(in_vmem(), in_vmem(), in_vmem()),
        compiler_params=pltpu.CompilerParams(vmem_limit_bytes=MIB),
        name="finish",
    )(kept, singular, mine, theirs)
    return tilde.T[None], proj.T[None], inter[None]


def solution(mesh):
    placed = (
        P("sec", "row", None),
        P("sec", None, None),
        P("sec", "row", None),
        P("sec", None, None),
        P("sec", "row", None),
        P("sec", "row", None),
        P("sec", None),
        P("sec"),
        P("sec"),
        P("sec", None),
    )
    return jax.shard_map(
        functools.partial(local, mesh.shape["sec"], mesh.shape["row"]),
        mesh=mesh,
        in_specs=placed,
        out_specs=(P("sec", "row", None), P("sec", "row", None), P("sec", None, None)),
        check_vma=False,
    )
```

```python
import functools

import jax
import jax.numpy as jnp
from jax import lax
from jax.experimental import pallas as pl
from jax.experimental.pallas import tpu as pltpu
from jax.sharding import PartitionSpec as P

LANES = 128
F32, BF16 = jnp.float32, jnp.bfloat16
MIB = 1024 * 1024
START_FLOPS = 2 * 10**9
JOIN_FLOPS = 10**10
FACTOR_FIRST = (1, 1)
RESULT_FIRST = (1, 1)


def iota(shape, dim):
    return lax.broadcasted_iota(jnp.int32, shape, dim)


def is_upper():
    return lax.axis_index("row") & 1 == 1


def start_kernel(out_ref):
    out_ref[...] = jnp.zeros(out_ref.shape, F32)


def own_kernel(after_ref, map_ref, u_ref, v_ref, own_ref, mover_ref):
    states_here = map_ref.shape[1]
    own_ref[...] = jnp.where(is_upper(), u_ref[...], v_ref[...])
    small = (states_here, states_here)
    entries = jnp.where(iota(small, 0) == iota(small, 1), map_ref[...].astype(F32), 0.0)
    entries = jnp.sum(entries, axis=1, keepdims=True).astype(jnp.int32)
    entries = jnp.broadcast_to(entries, (states_here, LANES))
    square = (LANES, LANES)
    wanted = jnp.concatenate([entries] * (LANES // states_here), axis=0) + iota(square, 0) // states_here * states_here
    mover_ref[...] = jnp.where(iota(square, 1) == wanted, 1.0, 0.0).astype(BF16)


def join_kernel(own_ref, mover_ref, u_got_ref, v_got_ref, out_ref):
    keep_cols, rows = u_got_ref.shape
    upper = is_upper()
    own = own_ref[...]
    got = jnp.where(upper, u_got_ref[...], v_got_ref[...])
    both = jnp.concatenate([jnp.where(upper, got, own), jnp.where(upper, own, got)], axis=1)
    starts = range(0, 2 * rows, LANES)
    stacked = jnp.concatenate([both[:, start : start + LANES] for start in starts], axis=0)
    moved = jnp.dot(stacked, mover_ref[...], preferred_element_type=F32).astype(BF16)
    for i, start in enumerate(starts):
        out_ref[:, start : start + LANES] = moved[i * keep_cols : (i + 1) * keep_cols]


def half_kernel(states_ref, ul, ul_got, ur, dl, dl_got, dr, out_ref, *, states_here):
    rows, width = ul.shape
    step = 2 * LANES
    group = LANES // states_here
    lane = iota((1, LANES), 1)
    chunk_shape = (states_here, LANES)
    live_rows = iota(chunk_shape, 0) < states_ref[0]
    live = live_rows & (iota(chunk_shape, 1) % states_here < states_ref[0])
    odd = {distance: (lane // states_here // distance) % 2 == 1 for distance in range(1, group)}

    def regroup(block):
        chunks = [block[i * states_here : (i + 1) * states_here] for i in range(group)]
        distance = 1
        while distance < group:
            shift = distance * states_here
            moved = list(chunks)
            for i in range(group):
                if i & distance == 0:
                    low, high = chunks[i], chunks[i + distance]
                    moved[i] = jnp.where(odd[distance], pltpu.roll(high, shift, 1), low)
                    moved[i + distance] = jnp.where(odd[distance], high, pltpu.roll(low, LANES - shift, 1))
            chunks = moved
            distance *= 2
        return chunks

    def work(first, second, matrix):
        if rows % LANES:
            lefts = [(0, jnp.concatenate([first[...], second[...]], axis=0))]
        else:
            lefts = [(0, first[...]), (rows, second[...])]
        for column in range(0, width, step):
            for base, left in lefts:
                full = jnp.dot(left, matrix[:, column : column + step], preferred_element_type=F32)
                for p in range(0, left.shape[0], LANES):
                    for q in range(0, step, LANES):
                        for i, chunk in enumerate(regroup(full[p : p + LANES, q : q + LANES])):
                            at = column + q + i * states_here
                            chunk = jnp.where(live, chunk, 0.0).astype(BF16)
                            out_ref[at : at + states_here, base + p : base + p + LANES] = chunk

    upper = is_upper()

    @pl.when(upper)
    def _():
        work(ul_got, ul, ur)

    @pl.when(jnp.logical_not(upper))
    def _():
        work(dl, dl_got, dr)


def apply_kernel(*refs):
    *factors, half_ref, out_ref = refs
    chips = len(factors)
    chip = lax.axis_index("row") // 2
    depth = factors[0].shape[1]
    total = jnp.zeros(out_ref.shape, F32)
    first = jnp.where(is_upper(), FACTOR_FIRST[1], FACTOR_FIRST[0])
    for turn in range(chips):
        source = lax.rem(chip - turn - first + 2 * chips, chips)
        part = half_ref[pl.ds(pl.multiple_of(source * depth, depth), depth), :]
        total += jnp.dot(factors[turn][...], part, preferred_element_type=F32)
    out_ref[...] = total.astype(BF16)


def finish_kernel(kept_ref, singular_ref, mine_ref, got_ref, tilde_ref, proj_ref, inter_ref, *, width, chips):
    keep_cols, rows = tilde_ref.shape
    core = lax.axis_index("row") % 2
    chip = lax.axis_index("row") // 2
    upper = is_upper()
    weight = jnp.where(iota((1, keep_cols), 1) < kept_ref[0], 1.0 / jnp.sqrt(singular_ref[...]), 0.0)
    square = (keep_cols, keep_cols)
    diagonal = iota(square, 0) == iota(square, 1)
    weight_rows = jnp.sum(jnp.where(diagonal, weight, 0.0), axis=1, keepdims=True)
    turns = [pl.ds(turn * keep_cols, keep_cols) for turn in range(chips)]
    lower_parts = [jnp.where(upper, got_ref[turn], mine_ref[turn]) for turn in turns]
    upper_parts = [jnp.where(upper, mine_ref[turn], got_ref[turn]) for turn in turns]
    lower_parts = [lower_parts[(away - RESULT_FIRST[0]) % chips] for away in range(chips)]
    upper_parts = [upper_parts[(away - RESULT_FIRST[1]) % chips] for away in range(chips)]
    for whole, ref in ((upper_parts[0], tilde_ref), (lower_parts[0], proj_ref)):
        own = jnp.where(core == 0, whole[:, :rows], whole[:, rows:])
        ref[...] = (own.astype(F32) * weight_rows).astype(BF16)
    products = [
        lax.dot_general(a, b, (((1,), (1,)), ((), ())), preferred_element_type=F32)
        for a, b in zip(upper_parts, lower_parts)
    ]
    total = products[0]
    if chips == 2:
        total = products[0] + products[1]
    elif chips > 2:
        total = jnp.zeros(square, F32)
        for source in range(chips):
            for away in range(chips):
                here = lax.rem(chip - away + chips, chips) == source
                total += jnp.where(here, products[away], 0.0)
    inter_ref[...] = total * (weight_rows * weight / jnp.sqrt(jnp.float32(width)))


def in_vmem():
    return pl.BlockSpec(memory_space=pltpu.VMEM)


def local(
    sectors,
    row_devices,
    corner_ul,
    corner_ur,
    corner_dl,
    corner_dr,
    left_factor,
    right_factor,
    singular,
    states,
    kept,
    joining_map,
):
    rows, width = corner_ul.shape[1:]
    states_here = joining_map.shape[1]
    keep_cols = left_factor.shape[2]
    chips = row_devices // 2

    def other_core(value):
        return lax.ppermute(value, "row", [(i, i ^ 1) for i in range(row_devices)])

    def to_sector(value, upper_step, turn, first):
        pairs = []
        for s in range(sectors):
            for r in range(row_devices):
                t = (s + (upper_step if r % 2 else -upper_step)) % sectors
                away = (turn + first[r % 2]) % chips
                pairs.append((s * row_devices + r, t * row_devices + (r + 2 * away) % row_devices))
        return lax.ppermute(value, ("sec", "row"), pairs)

    block = jax.ShapeDtypeStruct((keep_cols, rows), BF16)
    whole = jax.ShapeDtypeStruct((keep_cols, 2 * rows), BF16)
    u, v = left_factor[0].T, right_factor[0].T
    u_got, v_got = other_core(u), other_core(v)
    waited = pl.pallas_call(
        start_kernel,
        out_shape=jax.ShapeDtypeStruct((8, LANES), F32),
        in_specs=[],
        out_specs=in_vmem(),
        compiler_params=pltpu.CompilerParams(vmem_limit_bytes=MIB),
        cost_estimate=pl.CostEstimate(flops=START_FLOPS, bytes_accessed=0, transcendentals=0),
        name="start",
    )()
    own, mover = pl.pallas_call(
        own_kernel,
        out_shape=(block, jax.ShapeDtypeStruct((LANES, LANES), BF16)),
        in_specs=[in_vmem()] * 4,
        out_specs=(in_vmem(), in_vmem()),
        compiler_params=pltpu.CompilerParams(vmem_limit_bytes=MIB),
        name="own_factor",
    )(waited, joining_map, u, v)
    joined = pl.pallas_call(
        join_kernel,
        out_shape=whole,
        in_specs=[in_vmem()] * 4,
        out_specs=in_vmem(),
        compiler_params=pltpu.CompilerParams(vmem_limit_bytes=MIB),
        cost_estimate=pl.CostEstimate(flops=JOIN_FLOPS, bytes_accessed=0, transcendentals=0),
        name="join_factor",
    )(own, mover, u_got, v_got)
    factors = [to_sector(joined, -1, turn, FACTOR_FIRST) for turn in range(chips)]

    ul, dl = corner_ul[0], corner_dl[0]
    ul_got, dl_got = other_core(ul), other_core(dl)
    half = pl.pallas_call(
        functools.partial(half_kernel, states_here=states_here),
        out_shape=jax.ShapeDtypeStruct((width, 2 * rows), BF16),
        in_specs=[pl.BlockSpec(memory_space=pltpu.SMEM)] + [in_vmem()] * 6,
        out_specs=in_vmem(),
        compiler_params=pltpu.CompilerParams(vmem_limit_bytes=16 * MIB),
        cost_estimate=pl.CostEstimate(
            flops=rows * width, bytes_accessed=rows, transcendentals=0
        ),
        name="half_product",
    )(states, ul, ul_got, corner_ur[0], dl, dl_got, corner_dr[0])

    applied = pl.pallas_call(
        apply_kernel,
        out_shape=whole,
        in_specs=[in_vmem()] * (chips + 1),
        out_specs=in_vmem(),
        compiler_params=pltpu.CompilerParams(vmem_limit_bytes=4 * MIB),
        name="apply_factor",
    )(*factors, half)
    mine = [to_sector(applied, 1, turn, RESULT_FIRST) for turn in range(chips)]
    mine = jnp.concatenate(mine, axis=0)
    theirs = other_core(mine)

    tilde, proj, inter = pl.pallas_call(
        functools.partial(finish_kernel, width=width, chips=chips),
        out_shape=(block, block, jax.ShapeDtypeStruct((keep_cols, keep_cols), F32)),
        in_specs=[pl.BlockSpec(memory_space=pltpu.SMEM)] + [in_vmem()] * 3,
        out_specs=(in_vmem(), in_vmem(), in_vmem()),
        compiler_params=pltpu.CompilerParams(vmem_limit_bytes=MIB),
        name="finish",
    )(kept, singular, mine, theirs)
    return tilde.T[None], proj.T[None], inter[None]


def solution(mesh):
    placed = (
        P("sec", "row", None),
        P("sec", None, None),
        P("sec", "row", None),
        P("sec", None, None),
        P("sec", "row", None),
        P("sec", "row", None),
        P("sec", None),
        P("sec"),
        P("sec"),
        P("sec", None),
    )
    return jax.shard_map(
        functools.partial(local, mesh.shape["sec"], mesh.shape["row"]),
        mesh=mesh,
        in_specs=placed,
        out_specs=(P("sec", "row", None), P("sec", "row", None), P("sec", None, None)),
        check_vma=False,
    )
```

```python
import functools

import jax
import jax.numpy as jnp
from jax import lax
from jax.experimental import pallas as pl
from jax.experimental.pallas import tpu as pltpu
from jax.sharding import PartitionSpec as P

LANES = 128
F32, BF16 = jnp.float32, jnp.bfloat16
MIB = 1024 * 1024
START_FLOPS = 2 * 10**9
JOIN_FLOPS = 10**10
FACTOR_FIRST = (1, 1)
RESULT_FIRST = (1, 1)
FACTOR_WRAP = (1, 0)
RESULT_WRAP = (1, 1)


def iota(shape, dim):
    return lax.broadcasted_iota(jnp.int32, shape, dim)


def is_upper():
    return lax.axis_index("row") & 1 == 1


def start_kernel(out_ref):
    out_ref[...] = jnp.zeros(out_ref.shape, F32)


def own_kernel(after_ref, map_ref, u_ref, v_ref, own_ref, mover_ref):
    states_here = map_ref.shape[1]
    own_ref[...] = jnp.where(is_upper(), u_ref[...], v_ref[...])
    small = (states_here, states_here)
    entries = jnp.where(iota(small, 0) == iota(small, 1), map_ref[...].astype(F32), 0.0)
    entries = jnp.sum(entries, axis=1, keepdims=True).astype(jnp.int32)
    entries = jnp.broadcast_to(entries, (states_here, LANES))
    square = (LANES, LANES)
    wanted = jnp.concatenate([entries] * (LANES // states_here), axis=0) + iota(square, 0) // states_here * states_here
    mover_ref[...] = jnp.where(iota(square, 1) == wanted, 1.0, 0.0).astype(BF16)


def join_kernel(own_ref, mover_ref, u_got_ref, v_got_ref, out_ref):
    keep_cols, rows = u_got_ref.shape
    upper = is_upper()
    own = own_ref[...]
    got = jnp.where(upper, u_got_ref[...], v_got_ref[...])
    both = jnp.concatenate([jnp.where(upper, got, own), jnp.where(upper, own, got)], axis=1)
    starts = range(0, 2 * rows, LANES)
    stacked = jnp.concatenate([both[:, start : start + LANES] for start in starts], axis=0)
    moved = jnp.dot(stacked, mover_ref[...], preferred_element_type=F32).astype(BF16)
    for i, start in enumerate(starts):
        out_ref[:, start : start + LANES] = moved[i * keep_cols : (i + 1) * keep_cols]


def half_kernel(states_ref, ul, ul_got, ur, dl, dl_got, dr, out_ref, *, states_here):
    rows, width = ul.shape
    step = 2 * LANES
    group = LANES // states_here
    lane = iota((1, LANES), 1)
    chunk_shape = (states_here, LANES)
    live_rows = iota(chunk_shape, 0) < states_ref[0]
    live = live_rows & (iota(chunk_shape, 1) % states_here < states_ref[0])
    odd = {distance: (lane // states_here // distance) % 2 == 1 for distance in range(1, group)}

    def regroup(block):
        chunks = [block[i * states_here : (i + 1) * states_here] for i in range(group)]
        distance = 1
        while distance < group:
            shift = distance * states_here
            moved = list(chunks)
            for i in range(group):
                if i & distance == 0:
                    low, high = chunks[i], chunks[i + distance]
                    moved[i] = jnp.where(odd[distance], pltpu.roll(high, shift, 1), low)
                    moved[i + distance] = jnp.where(odd[distance], high, pltpu.roll(low, LANES - shift, 1))
            chunks = moved
            distance *= 2
        return chunks

    def work(first, second, matrix):
        if rows % LANES:
            lefts = [(0, jnp.concatenate([first[...], second[...]], axis=0))]
        else:
            lefts = [(0, first[...]), (rows, second[...])]
        for column in range(0, width, step):
            for base, left in lefts:
                full = jnp.dot(left, matrix[:, column : column + step], preferred_element_type=F32)
                for p in range(0, left.shape[0], LANES):
                    for q in range(0, step, LANES):
                        for i, chunk in enumerate(regroup(full[p : p + LANES, q : q + LANES])):
                            at = column + q + i * states_here
                            chunk = jnp.where(live, chunk, 0.0).astype(BF16)
                            out_ref[at : at + states_here, base + p : base + p + LANES] = chunk

    upper = is_upper()

    @pl.when(upper)
    def _():
        work(ul_got, ul, ur)

    @pl.when(jnp.logical_not(upper))
    def _():
        work(dl, dl_got, dr)


def apply_kernel(*refs):
    *factors, half_ref, out_ref = refs
    chips = len(factors)
    chip = lax.axis_index("row") // 2
    depth = factors[0].shape[1]
    total = jnp.zeros(out_ref.shape, F32)
    sector, last = lax.axis_index("sec"), lax.axis_size("sec") - 1
    first = jnp.where(
        is_upper(),
        jnp.where(sector == last, FACTOR_WRAP[1], FACTOR_FIRST[1]),
        jnp.where(sector == 0, FACTOR_WRAP[0], FACTOR_FIRST[0]),
    )
    for turn in range(chips):
        source = lax.rem(chip - turn - first + 2 * chips, chips)
        part = half_ref[pl.ds(pl.multiple_of(source * depth, depth), depth), :]
        total += jnp.dot(factors[turn][...], part, preferred_element_type=F32)
    out_ref[...] = total.astype(BF16)


def finish_kernel(kept_ref, singular_ref, mine_ref, got_ref, tilde_ref, proj_ref, inter_ref, *, width, chips):
    keep_cols, rows = tilde_ref.shape
    core = lax.axis_index("row") % 2
    chip = lax.axis_index("row") // 2
    upper = is_upper()
    weight = jnp.where(iota((1, keep_cols), 1) < kept_ref[0], 1.0 / jnp.sqrt(singular_ref[...]), 0.0)
    square = (keep_cols, keep_cols)
    diagonal = iota(square, 0) == iota(square, 1)
    weight_rows = jnp.sum(jnp.where(diagonal, weight, 0.0), axis=1, keepdims=True)
    turns = [pl.ds(turn * keep_cols, keep_cols) for turn in range(chips)]
    lower_parts = [jnp.where(upper, got_ref[turn], mine_ref[turn]) for turn in turns]
    upper_parts = [jnp.where(upper, mine_ref[turn], got_ref[turn]) for turn in turns]
    sector, last = lax.axis_index("sec"), lax.axis_size("sec") - 1

    def ordered(parts, core, wraps):
        found = []
        for away in range(chips):
            usual = parts[(away - RESULT_FIRST[core]) % chips]
            wrapped = parts[(away - RESULT_WRAP[core]) % chips]
            found.append(jnp.where(wraps, wrapped, usual))
        return found

    lower_parts = ordered(lower_parts, 0, sector == last)
    upper_parts = ordered(upper_parts, 1, sector == 0)
    for whole, ref in ((upper_parts[0], tilde_ref), (lower_parts[0], proj_ref)):
        own = jnp.where(core == 0, whole[:, :rows], whole[:, rows:])
        ref[...] = (own.astype(F32) * weight_rows).astype(BF16)
    products = [
        lax.dot_general(a, b, (((1,), (1,)), ((), ())), preferred_element_type=F32)
        for a, b in zip(upper_parts, lower_parts)
    ]
    total = products[0]
    if chips == 2:
        total = products[0] + products[1]
    elif chips > 2:
        total = jnp.zeros(square, F32)
        for source in range(chips):
            for away in range(chips):
                here = lax.rem(chip - away + chips, chips) == source
                total += jnp.where(here, products[away], 0.0)
    inter_ref[...] = total * (weight_rows * weight / jnp.sqrt(jnp.float32(width)))


def in_vmem():
    return pl.BlockSpec(memory_space=pltpu.VMEM)


def local(
    sectors,
    row_devices,
    corner_ul,
    corner_ur,
    corner_dl,
    corner_dr,
    left_factor,
    right_factor,
    singular,
    states,
    kept,
    joining_map,
):
    rows, width = corner_ul.shape[1:]
    states_here = joining_map.shape[1]
    keep_cols = left_factor.shape[2]
    chips = row_devices // 2

    def other_core(value):
        return lax.ppermute(value, "row", [(i, i ^ 1) for i in range(row_devices)])

    def to_sector(value, upper_step, turn, first, wrap):
        pairs = []
        for s in range(sectors):
            for r in range(row_devices):
                t = s + (upper_step if r % 2 else -upper_step)
                away = (turn + (first if 0 <= t < sectors else wrap)[r % 2]) % chips
                pairs.append((s * row_devices + r, t % sectors * row_devices + (r + 2 * away) % row_devices))
        return lax.ppermute(value, ("sec", "row"), pairs)

    block = jax.ShapeDtypeStruct((keep_cols, rows), BF16)
    whole = jax.ShapeDtypeStruct((keep_cols, 2 * rows), BF16)
    u, v = left_factor[0].T, right_factor[0].T
    u_got, v_got = other_core(u), other_core(v)
    waited = pl.pallas_call(
        start_kernel,
        out_shape=jax.ShapeDtypeStruct((8, LANES), F32),
        in_specs=[],
        out_specs=in_vmem(),
        compiler_params=pltpu.CompilerParams(vmem_limit_bytes=MIB),
        cost_estimate=pl.CostEstimate(flops=START_FLOPS, bytes_accessed=0, transcendentals=0),
        name="start",
    )()
    own, mover = pl.pallas_call(
        own_kernel,
        out_shape=(block, jax.ShapeDtypeStruct((LANES, LANES), BF16)),
        in_specs=[in_vmem()] * 4,
        out_specs=(in_vmem(), in_vmem()),
        compiler_params=pltpu.CompilerParams(vmem_limit_bytes=MIB),
        name="own_factor",
    )(waited, joining_map, u, v)
    joined = pl.pallas_call(
        join_kernel,
        out_shape=whole,
        in_specs=[in_vmem()] * 4,
        out_specs=in_vmem(),
        compiler_params=pltpu.CompilerParams(vmem_limit_bytes=MIB),
        cost_estimate=pl.CostEstimate(flops=JOIN_FLOPS, bytes_accessed=0, transcendentals=0),
        name="join_factor",
    )(own, mover, u_got, v_got)
    factors = [to_sector(joined, -1, turn, FACTOR_FIRST, FACTOR_WRAP) for turn in range(chips)]

    ul, dl = corner_ul[0], corner_dl[0]
    ul_got, dl_got = other_core(ul), other_core(dl)
    half = pl.pallas_call(
        functools.partial(half_kernel, states_here=states_here),
        out_shape=jax.ShapeDtypeStruct((width, 2 * rows), BF16),
        in_specs=[pl.BlockSpec(memory_space=pltpu.SMEM)] + [in_vmem()] * 6,
        out_specs=in_vmem(),
        compiler_params=pltpu.CompilerParams(vmem_limit_bytes=16 * MIB),
        cost_estimate=pl.CostEstimate(
            flops=rows * width, bytes_accessed=rows, transcendentals=0
        ),
        name="half_product",
    )(states, ul, ul_got, corner_ur[0], dl, dl_got, corner_dr[0])

    applied = pl.pallas_call(
        apply_kernel,
        out_shape=whole,
        in_specs=[in_vmem()] * (chips + 1),
        out_specs=in_vmem(),
        compiler_params=pltpu.CompilerParams(vmem_limit_bytes=4 * MIB),
        name="apply_factor",
    )(*factors, half)
    mine = [to_sector(applied, 1, turn, RESULT_FIRST, RESULT_WRAP) for turn in range(chips)]
    mine = jnp.concatenate(mine, axis=0)
    theirs = other_core(mine)

    tilde, proj, inter = pl.pallas_call(
        functools.partial(finish_kernel, width=width, chips=chips),
        out_shape=(block, block, jax.ShapeDtypeStruct((keep_cols, keep_cols), F32)),
        in_specs=[pl.BlockSpec(memory_space=pltpu.SMEM)] + [in_vmem()] * 3,
        out_specs=(in_vmem(), in_vmem(), in_vmem()),
        compiler_params=pltpu.CompilerParams(vmem_limit_bytes=MIB),
        name="finish",
    )(kept, singular, mine, theirs)
    return tilde.T[None], proj.T[None], inter[None]


def solution(mesh):
    placed = (
        P("sec", "row", None),
        P("sec", None, None),
        P("sec", "row", None),
        P("sec", None, None),
        P("sec", "row", None),
        P("sec", "row", None),
        P("sec", None),
        P("sec"),
        P("sec"),
        P("sec", None),
    )
    return jax.shard_map(
        functools.partial(local, mesh.shape["sec"], mesh.shape["row"]),
        mesh=mesh,
        in_specs=placed,
        out_specs=(P("sec", "row", None), P("sec", "row", None), P("sec", None, None)),
        check_vma=False,
    )
```
